128 devices in a mesh: outer: 8 (over x_hi, y), inner: 16 (over z, x_lo, core).
Axes of the slice: x: 4 (x_hi: 2, x_lo: 2; x = x_hi * 2 + x_lo), y: 4, z: 4, core: 2. Of those that a mesh axis runs over, the one named last changes fastest.
Arguments:
- image_codes: int32 [24576, 768], P(('outer', 'inner')), may hold values from 32 to 207, as said below
- image_exps: int32 [24576, 6], P(('outer', 'inner')), may hold values from -8 to -4
- text_codes: int32 [24576, 768], P(('outer', 'inner')), may hold values from 32 to 207, as said below
- text_exps: int32 [24576, 6], P(('outer', 'inner')), may hold values from -8 to -4
- logit_scale: float32 [1], replicated, may hold values from 20 to 100
Outputs:
- mean_loss: float32 [], replicated
- image_grad: float32 [24576, 768], P(('outer', 'inner'))
- text_grad: float32 [24576, 768], P(('outer', 'inner'))
The draws below stay inside these ranges and needn't reach their ends.
Inputs may be any that keep to these rules, and one draw needn't show every extreme that they name: `image_codes`: each code is an e4m3 byte: sign in bit 7, exponent field in bits 3 to 6, mantissa in bits 0 to 2; the exponent field is never 0 or 15. `text_codes`: each code is an e4m3 byte: sign in bit 7, exponent field in bits 3 to 6, mantissa in bits 0 to 2; the exponent field is never 0 or 15.
All inputs are finite; a program needn't handle non-finite values.
Results may differ from the reference program's by a relative error of at most 0.002.
Values may be sent and summed in bfloat16 or wider, within the bound.
A program may use at most 128 MiB of HBM per device.

```python
import math
import jax
import jax.numpy as jnp
from jax import lax

ROWS_DEV = 192
D = 768
NBLK = 6
PAIRS = 24576
N_INNER = 16


def drawn_rows():
    row_index = jnp.arange(PAIRS, dtype=jnp.int32)
    return row_index % 64 == 7


def code_pair(key):
    subkeys = jax.random.split(key, 7)
    full_shape = (PAIRS, D)
    image_part = jax.random.randint(subkeys[0], full_shape, 0, 2) * 128 + jax.random.randint(subkeys[1], full_shape, 4, 10) * 8 + jax.random.randint(subkeys[2], full_shape, 0, 8)
    fresh_codes = jax.random.randint(subkeys[3], full_shape, 0, 2) * 128 + jax.random.randint(subkeys[4], full_shape, 4, 10) * 8 + jax.random.randint(subkeys[5], full_shape, 0, 8)
    copied = jax.random.randint(subkeys[6], full_shape, 0, 10) < 2
    copied = jnp.logical_or(copied, drawn_rows()[:, None])
    return (image_part, jnp.where(copied, image_part, fresh_codes))


def scale_exponents(key):
    row_keys = jax.random.split(key, 2)
    rising = 2 * jnp.arange(PAIRS, dtype=jnp.int32) // PAIRS
    per_row = jax.random.randint(row_keys[0], (PAIRS, 1), 0, 2)
    per_block = jax.random.randint(row_keys[1], (PAIRS, NBLK), 0, 2)
    base = rising[:, None] + per_row + per_block - 8
    row_index = jnp.arange(PAIRS, dtype=jnp.int32)
    strength = jnp.where(row_index // 64 % 2 == 0, -4, -5)
    planted = jnp.where(drawn_rows()[:, None], strength[:, None], base)
    return planted.astype(jnp.int32)


def draw_image_codes(key, part):
    return code_pair(key)[0].astype(jnp.int32)


def draw_text_codes(key, part):
    return code_pair(key)[1].astype(jnp.int32)


def draw_image_exps(key, part):
    key = jax.random.fold_in(key, 11)
    return scale_exponents(key)


def draw_text_exps(key, part):
    key = jax.random.fold_in(key, 13)
    return scale_exponents(key)


def draw_logit_scale(key, part):
    key = jax.random.fold_in(key, 17)
    return jnp.exp(jax.random.uniform(key, (1,), jnp.float32, math.log(20.0), math.log(100.0)))


def setup_inputs(seed: int = 0) -> dict:
    seeds = jax.random.split(jax.random.key(seed), 6)
    return {
        "image_codes": draw_image_codes(jax.random.fold_in(seeds[5], 71), 0),
        "image_exps": draw_image_exps(jax.random.fold_in(seeds[5], 71), 0),
        "text_codes": draw_text_codes(jax.random.fold_in(seeds[5], 71), 0),
        "text_exps": draw_text_exps(jax.random.fold_in(seeds[5], 71), 0),
        "logit_scale": draw_logit_scale(jax.random.fold_in(seeds[5], 71), 0),
    }


MANT_UNIT = 2.0 ** -9


def decode(code_values, exponents):
    sign_bit = code_values // 128
    exp_field = (code_values // 8) % 16
    mantissa = code_values % 8
    significand = jnp.where(exp_field > 0, mantissa + 8, mantissa)
    power_int = jnp.left_shift(jnp.int32(1), jnp.maximum(exp_field, 1) - 1)
    magnitude = (significand * power_int).astype(jnp.float32) * MANT_UNIT
    signed_value = jnp.where(sign_bit > 0, -magnitude, magnitude)
    divisor = jnp.left_shift(jnp.int32(1), -exponents).astype(jnp.float32)
    row_count, feature_count = code_values.shape
    blocks = exponents.shape[1]
    shaped = signed_value.reshape(row_count, blocks, feature_count // blocks) / divisor[:, :, None]
    return shaped.reshape(row_count, feature_count).astype(jnp.bfloat16)


def reference(image_codes, image_exps, text_codes, text_exps, logit_scale):
    images = decode(image_codes, image_exps)
    text_rows = decode(text_codes, text_exps)
    logit_mult = logit_scale[0]
    image_wide = images.astype(jnp.float32)
    text_wide = text_rows.astype(jnp.float32)
    total_rows = images.shape[0]
    group_rows = ROWS_DEV * N_INNER
    text_blocks = text_wide.reshape(total_rows // group_rows, group_rows, D)
    contract_last = (((1,), (1,)), ((), ()))

    def first_pass(running, text_block):
        row_max, row_sum = running
        score_block = logit_mult * lax.dot_general(text_block, image_wide, contract_last, preferred_element_type=jnp.float32)
        col_max = jnp.max(score_block, axis=1)
        col_lse = col_max + jnp.log(jnp.sum(jnp.exp(score_block - col_max[:, None]), axis=1))
        highest = jnp.maximum(row_max, jnp.max(score_block, axis=0))
        row_sum = row_sum * jnp.exp(row_max - highest) + jnp.sum(jnp.exp(score_block - highest[None, :]), axis=0)
        return (highest, row_sum), col_lse

    initial = (jnp.full((total_rows,), -jnp.inf, jnp.float32), jnp.zeros((total_rows,), jnp.float32))
    (row_max, row_sum), col_parts = lax.scan(first_pass, initial, text_blocks)
    row_lse = row_max + jnp.log(row_sum)
    col_lse = col_parts.reshape(total_rows)
    diagonal = logit_mult * jnp.sum(image_wide * text_wide, axis=1)
    mean_loss = jnp.sum(row_lse + col_lse - 2.0 * diagonal) / (2 * total_rows)

    def second_pass(image_acc, pieces):
        text_block, block_lse = pieces
        score_block = logit_mult * lax.dot_general(text_block, image_wide, contract_last, preferred_element_type=jnp.float32)
        weights = ((jnp.exp(score_block - block_lse[:, None]) + jnp.exp(score_block - row_lse[None, :])) * 0.5).astype(jnp.bfloat16)
        weights = lax.optimization_barrier(weights).astype(jnp.float32)
        text_part = jnp.dot(weights, image_wide, preferred_element_type=jnp.float32)
        image_acc = image_acc + lax.dot_general(weights, text_block, (((0,), (0,)), ((), ())), preferred_element_type=jnp.float32)
        return image_acc, text_part

    image_acc, text_parts = lax.scan(second_pass, jnp.zeros((total_rows, D), jnp.float32), (text_blocks, col_parts))
    image_grad = logit_mult * (image_acc - text_wide)
    text_grad = logit_mult * (text_parts.reshape(total_rows, D) - image_wide)
    return mean_loss, image_grad, text_grad
```

```python
import functools

import jax
import jax.numpy as jnp
from jax import lax
from jax.experimental import pallas as pl
from jax.experimental.pallas import tpu as pltpu
from jax.sharding import PartitionSpec as P

LOG2E = 1.4426950408889634
LN2 = 0.6931471805599453
UNIT = 2.0 ** -17
LOW = -1e30
Z_OFF = (0, 1, 3, 2)
GROUP = {off: g for g, off in enumerate(Z_OFF)}
SLOTS = ((0, 0), (0, 1), (0, 3), (1, 0), (0, 2), (1, 1), (1, 3), (1, 2))
SLOT = {pos: s for s, pos in enumerate(SLOTS)}
INNER = [(r, a, b) for r in range(4) for a in range(2) for b in range(2)]
MESSAGES = (
    ["tx", "ix", "xs", "xi"]
    + [f"tc{r}{a}" for r in range(4) for a in range(2)]
    + [f"{n}{d}{a}" for n in ("tz", "th", "iy", "ih", "zf", "yf") for d in "pm" for a in range(2)]
    + [f"{n}{d}" for n in ("zh", "yh") for d in "pm"]
    + [f"cs{g}" for g in range(4)]
    + [f"{n}{s}" for n in ("lr", "lo") for s in range(1, 8)]
    + [f"{n}{q}" for n in ("lc", "li") for q in range(1, 16)]
)
SEM = {name: i for i, name in enumerate(MESSAGES)}


def dot_nt(a, b):
    return lax.dot_general(a, b, (((1,), (1,)), ((), ())), preferred_element_type=jnp.float32)


def dot_nn(a, b):
    return jnp.dot(a, b, preferred_element_type=jnp.float32)


def dot_tn(a, b):
    return lax.dot_general(a, b, (((0,), (0,)), ((), ())), preferred_element_type=jnp.float32)


def kernel(
    ic_ref, ie_ref, tc_ref, te_ref, scale_ref, loss_ref, ig_ref, tg_ref,
    T, I, S, W, mr, sr, mc, sc, lrep, lcol, LR, LC, LO, LI,
    CS, CR, ZS, ZH, ZF, YS, YH, YF, XS, XR, dsum, send_sems, recv_sems,
):
    R, D = ic_ref.shape
    H = R // 2
    G = 4 * R
    RP = LR.shape[2]
    NT = G // 128
    ND = D // 128

    outer = lax.axis_index("outer")
    inner = lax.axis_index("inner")
    xh, y = outer // 4, outer % 4
    z, xl, c = inner // 4, (inner // 2) % 2, inner % 2

    def at(dh=0, dy=0, dz=0, dl=0, dc=0):
        h = xh if dh == 0 else 1 - xh
        l = xl if dl == 0 else 1 - xl
        k = c if dc == 0 else 1 - c
        return (h * 4 + (y + dy) % 4, ((z + dz) % 4) * 4 + l * 2 + k)

    outer_peers = [(s, SLOTS[s]) for s in range(1, 8)]
    inner_peers = [(q, INNER[q]) for q in range(1, 16)]
    barrier = pltpu.get_barrier_semaphore()
    for _, (a, r) in outer_peers:
        pl.semaphore_signal(barrier, inc=1, device_id=at(dh=a, dy=r), device_id_type=pl.DeviceIdType.MESH)
    for _, (r, a, b) in inner_peers:
        pl.semaphore_signal(
            barrier, inc=1, device_id=at(dz=r, dl=a, dc=b), device_id_type=pl.DeviceIdType.MESH
        )

    def copy(name, src, dst, device):
        return pltpu.make_async_remote_copy(
            src_ref=src, dst_ref=dst, send_sem=send_sems.at[SEM[name]], recv_sem=recv_sems.at[SEM[name]],
            device_id=device, device_id_type=pl.DeviceIdType.MESH,
        )

    started = {}

    def send(name, src, dst, device):
        started[name] = copy(name, src, dst, device)
        started[name].start()

    def got(name):
        started[name].wait_recv()

    def trow(a, b):
        l = xl if a == 0 else 1 - xl
        k = c if b == 0 else 1 - c
        return pl.multiple_of((l * 2 + k) * R, R)

    def tblock(r, a, b=0):
        return T.at[GROUP[r], pl.ds(trow(a, b), R), :]

    def thalf(r, a, half):
        return T.at[GROUP[r], pl.ds(pl.multiple_of(trow(a, 0) + half * H, H), H), :]

    def iblock(a, r):
        return I.at[pl.ds(SLOT[a, r] * R, R), :]

    def ihalf(a, r, half):
        return I.at[pl.ds(SLOT[a, r] * R + half * H, H), :]

    def decode(codes_ref, exps_ref, f):
        codes = codes_ref[:, f * 128 : (f + 1) * 128]
        field = (codes >> 3) & 15
        mantissa = codes & 7
        significand = jnp.where(field > 0, mantissa + 8, mantissa)
        shift = jnp.maximum(field, 1) - 1 + (exps_ref[:, f : f + 1] + 8)
        magnitude = (significand << shift).astype(jnp.float32) * UNIT
        return jnp.where(codes > 127, -magnitude, magnitude)

    own_rows = trow(0, 0)
    diag = jnp.zeros((R, 128), jnp.float32)
    for f in range(ND):
        image = decode(ic_ref, ie_ref, f)
        text = decode(tc_ref, te_ref, f)
        diag = diag + image * text
        I[0:R, f * 128 : (f + 1) * 128] = image.astype(jnp.bfloat16)
        T[0, pl.ds(own_rows, R), f * 128 : (f + 1) * 128] = text.astype(jnp.bfloat16)
    dsum[0:R, :] = diag
    if RP > R:
        dsum[R:RP, :] = jnp.zeros((RP - R, 128), jnp.float32)
        for s in range(8):
            mr[s, R:RP, :] = jnp.zeros((RP - R, 128), jnp.float32)
            sr[s, R:RP, :] = jnp.ones((RP - R, 128), jnp.float32)
    for s in range(8):
        mr[s, 0:R, :] = jnp.full((R, 128), LOW, jnp.float32)
        sr[s, 0:R, :] = jnp.zeros((R, 128), jnp.float32)
    mc[...] = jnp.full(mc.shape, LOW, jnp.float32)
    sc[...] = jnp.zeros(sc.shape, jnp.float32)
    k = scale_ref[0]
    k2 = k * LOG2E

    pl.semaphore_wait(barrier, 22)

    def s_unit(g, slot):
        rows = pl.ds(pl.multiple_of(slot * R, R), R)
        tile = dot_nt(I[rows, :], T[g]) * k2
        S[g, rows, :] = tile
        parts = [tile[:, j * 128 : (j + 1) * 128] for j in range(NT)]
        old = mr[slot, 0:R, :]
        top = functools.reduce(jnp.maximum, parts, old)
        total = sr[slot, 0:R, :] * jnp.exp2(old - top)
        for part in parts:
            total = total + jnp.exp2(part - top)
        mr[slot, 0:R, :] = top
        sr[slot, 0:R, :] = total
        cols = tile.reshape(R // 8, 8, G)
        old = mc[g]
        top = jnp.maximum(old, jnp.max(cols, axis=0))
        sc[g] = sc[g] * jnp.exp2(old - top) + jnp.sum(jnp.exp2(cols - top[None]), axis=0)
        mc[g] = top

    def s_units(g, lo, hi):
        lax.fori_loop(lo, hi, lambda slot, _: (s_unit(g, slot), 0)[1], 0)

    send("tzm0", tblock(0, 0), tblock(3, 0), at(dz=1))
    send("tzp0", tblock(0, 0), tblock(1, 0), at(dz=3))
    send("iym0", iblock(0, 0), iblock(0, 3), at(dy=1))
    send("iyp0", iblock(0, 0), iblock(0, 1), at(dy=3))
    send("tx", tblock(0, 0), tblock(0, 0), at(dl=1))
    send("ix", iblock(0, 0), iblock(1, 0), at(dh=1))
    send("tc00", tblock(0, 0), tblock(0, 0), at(dc=1))

    def to_core(r, a):
        send(f"tc{r}{a}", tblock(r, a), tblock(r, a), at(dc=1))

    def forward(a):
        got(f"tzm{a}")
        send(f"thm{a}", thalf(3, a, 0), thalf(2, a, 0), at(dz=1))
        got(f"tzp{a}")
        send(f"thp{a}", thalf(1, a, 1), thalf(2, a, 1), at(dz=3))
        to_core(3, a)
        to_core(1, a)
        got(f"iym{a}")
        send(f"ihm{a}", ihalf(a, 3, 0), ihalf(a, 2, 0), at(dy=1))
        got(f"iyp{a}")
        send(f"ihp{a}", ihalf(a, 1, 1), ihalf(a, 2, 1), at(dy=3))

    def arrived(a):
        got(f"thm{a}")
        got(f"thp{a}")
        to_core(2, a)
        got(f"ihm{a}")
        got(f"ihp{a}")

    forward(0)
    got("tx")
    send("tzm1", tblock(0, 1), tblock(3, 1), at(dz=1))
    send("tzp1", tblock(0, 1), tblock(1, 1), at(dz=3))
    to_core(0, 1)
    got("ix")
    send("iym1", iblock(1, 0), iblock(1, 3), at(dy=1))
    send("iyp1", iblock(1, 0), iblock(1, 1), at(dy=3))
    got("tc00")
    got("tc01")
    s_units(0, 0, 4)
    arrived(0)
    s_units(0, 4, 5)
    forward(1)
    for name in ("tc10", "tc11", "tc30", "tc31"):
        got(name)
    s_units(0, 5, 7)
    s_units(1, 0, 7)
    s_units(2, 0, 7)
    arrived(1)
    s_units(0, 7, 8)
    s_units(1, 7, 8)
    s_units(2, 7, 8)
    got("tc20")
    got("tc21")
    s_units(3, 0, 8)

    for s in range(8):
        m = mr[s].T
        top = jnp.max(m, axis=0, keepdims=True)
        total = jnp.sum(sr[s].T * jnp.exp2(m - top), axis=0, keepdims=True)
        LR[0, s : s + 1, :] = top + jnp.log(total) * LOG2E
    for s, (a, r) in outer_peers:
        send(f"lr{s}", LR.at[0], LR.at[SLOT[a, -r % 4]], at(dh=a, dy=r))
    for g in range(4):
        m = mc[g]
        top = jnp.max(m, axis=0, keepdims=True)
        total = jnp.sum(sc[g] * jnp.exp2(m - top), axis=0, keepdims=True)
        LC[0, g : g + 1, :] = top + jnp.log(total) * LOG2E
    for q, (r, a, b) in inner_peers:
        send(f"lc{q}", LC.at[0], LC.at[INNER.index((-r % 4, a, b))], at(dz=r, dl=a, dc=b))

    def merge(parts):
        top = functools.reduce(jnp.maximum, parts)
        total = functools.reduce(jnp.add, [jnp.exp2(part - top) for part in parts])
        return top + jnp.log(total) * LOG2E

    for s, _ in outer_peers:
        got(f"lr{s}")
    row_own = None
    for s, (a, r) in enumerate(SLOTS):
        parts = []
        for p, (da, dr) in enumerate(SLOTS):
            there = SLOT[a ^ da, (r - dr) % 4]
            parts.append(LR[p, there : there + 1, :])
        lse = merge(parts)
        if s == 0:
            row_own = lse
        lrep[s] = jnp.broadcast_to(lse + 1.0, (128, RP)).T
    for q, _ in inner_peers:
        got(f"lc{q}")
    col_own = None
    for g, r in enumerate(Z_OFF):
        parts = []
        for q, (dr, _, _) in enumerate(INNER):
            there = GROUP[(r - dr) % 4]
            parts.append(LC[q, there : there + 1, :])
        lse = merge(parts)
        if g == 0:
            col_own = lse
        lcol[g] = jnp.broadcast_to(lse + 1.0, (8, G))

    block = xl * 2 + c
    col_mine = col_own[:, 0:R]
    for b in range(1, 4):
        col_mine = jnp.where(block == b, col_own[:, b * R : (b + 1) * R], col_mine)
    diag_own = jnp.sum(dsum[...].T, axis=0, keepdims=True)[:, 0:R] * k2
    loss_here = jnp.sum(row_own[:, 0:R] + col_mine - 2.0 * diag_own)
    LO[0] = jnp.full((8, 128), loss_here, jnp.float32)
    for s, (a, r) in outer_peers:
        send(f"lo{s}", LO.at[0], LO.at[SLOT[a, -r % 4]], at(dh=a, dy=r))

    def w_unit(g, slot):
        rows = pl.ds(pl.multiple_of(slot * R, R), R)
        by_row = lrep[slot, 0:R, :]
        for j in range(NT):
            cols = slice(j * 128, (j + 1) * 128)
            s = S[g, rows, cols]
            w = jnp.exp2(s - by_row) + jnp.exp2(s - lcol[g, 0:1, cols])
            W[g, rows, cols] = w.astype(jnp.bfloat16)

    def w_units(g, lo, hi):
        lax.fori_loop(lo, hi, lambda slot, _: (w_unit(g, slot), 0)[1], 0)

    TW = 384 if G % 384 == 0 else 128

    def t_terms(g):
        def step(j, _):
            cols = pl.ds(pl.multiple_of(j * TW, TW), TW)
            S[g, cols, :] = dot_tn(W[g, :, cols], I[...])
            return 0

        lax.fori_loop(0, G // TW, step, 0)
        for a in range(2):
            CS[g, a] = S[g, pl.ds(trow(a, 1), R), :].astype(jnp.bfloat16)
        send(f"cs{g}", CS.at[g], CR.at[g], at(dc=1))

    def t_sum(g, a):
        return S[g, pl.ds(trow(a, 0), R), :] + CR[g, a].astype(jnp.float32)

    def i_terms(slot):
        rows = slice(slot * R, (slot + 1) * R)
        total = dot_nn(W[0, rows, :], T[0])
        for g in range(1, 4):
            total = total + dot_nn(W[g, rows, :], T[g])
        return total

    w_units(3, 0, 8)
    t_terms(3)
    for g in range(3):
        w_units(g, 4, 5)
        w_units(g, 7, 8)
    for a in range(2):
        term = i_terms(SLOT[a, 2]).astype(jnp.bfloat16)
        YS[0, 0, a] = term[0:H]
        YS[0, 1, a] = term[H:R]
    send("yhm", YS.at[0, 0], YH.at[0], at(dy=1))
    send("yhp", YS.at[0, 1], YH.at[1], at(dy=3))
    got("cs3")
    for a in range(2):
        term = t_sum(3, a).astype(jnp.bfloat16)
        ZS[0, 0, a] = term[0:H]
        ZS[0, 1, a] = term[H:R]
    send("zhm", ZS.at[0, 0], ZH.at[0], at(dz=1))
    send("zhp", ZS.at[0, 1], ZH.at[1], at(dz=3))

    w_units(1, 0, 4)
    w_units(1, 5, 7)
    t_terms(1)
    w_units(2, 0, 4)
    w_units(2, 5, 7)
    t_terms(2)

    def near(index, half, a, term, held, out):
        for h in range(2):
            part = term[h * H : (h + 1) * H]
            if h == half:
                part = part + held[half, a].astype(jnp.float32)
            out[index, h, a] = part.astype(jnp.bfloat16)

    got("cs1")
    got("zhm")
    for a in (1, 0):
        near(1, 0, a, t_sum(1, a), ZH, ZS)
        send(f"zfm{a}", ZS.at[1, :, a], ZF.at[0, a], at(dz=1))
    got("cs2")
    got("zhp")
    for a in (1, 0):
        near(2, 1, a, t_sum(2, a), ZH, ZS)
        send(f"zfp{a}", ZS.at[2, :, a], ZF.at[1, a], at(dz=3))
    w_units(0, 0, 4)
    w_units(0, 5, 7)
    got("yhm")
    for a in (1, 0):
        near(1, 0, a, i_terms(SLOT[a, 1]), YH, YS)
        send(f"yfm{a}", YS.at[1, :, a], YF.at[0, a], at(dy=1))
    got("yhp")
    for a in (1, 0):
        near(2, 1, a, i_terms(SLOT[a, 3]), YH, YS)
        send(f"yfp{a}", YS.at[2, :, a], YF.at[1, a], at(dy=3))
    t_terms(0)

    for s, _ in outer_peers:
        got(f"lo{s}")

    def ring(values):
        return (values[0] + values[2]) + (values[1] + values[3])

    outer_loss = ring([LO[SLOT[0, r]] for r in range(4)]) + ring([LO[SLOT[1, r]] for r in range(4)])
    LI[0] = outer_loss
    for q, (r, a, b) in inner_peers:
        send(f"li{q}", LI.at[0], LI.at[INNER.index((-r % 4, a, b))], at(dz=r, dl=a, dc=b))

    ig_ref[...] = i_terms(SLOT[0, 0])
    far = i_terms(SLOT[1, 0])

    def both(held, a, term):
        halves = []
        for h in range(2):
            part = term[h * H : (h + 1) * H]
            halves.append(part + (held[0, a, h].astype(jnp.float32) + held[1, a, h].astype(jnp.float32)))
        return halves

    got("cs0")
    got("zfm1")
    got("zfp1")
    for h, part in enumerate(both(ZF, 1, t_sum(0, 1))):
        XS[0, h * H : (h + 1) * H, :] = part.astype(jnp.bfloat16)
    send("xs", XS.at[0], XR.at[0], at(dl=1))
    got("yfm1")
    got("yfp1")
    for h, part in enumerate(both(YF, 1, far)):
        XS[1, h * H : (h + 1) * H, :] = part.astype(jnp.bfloat16)
    send("xi", XS.at[1], XR.at[1], at(dh=1))

    for q, _ in inner_peers:
        got(f"li{q}")
    by_z = []
    for r in range(4):
        v = [[LI[INNER.index((r, a, b))] for b in range(2)] for a in range(2)]
        by_z.append((v[0][0] + v[0][1]) + (v[1][0] + v[1][1]))
    loss_ref[...] = ring(by_z) * (LN2 / (2 * 128 * R))

    got("zfm0")
    got("zfp0")
    text_parts = both(ZF, 0, t_sum(0, 0))
    got("xs")
    for h, part in enumerate(text_parts):
        rows = slice(h * H, (h + 1) * H)
        total = part + XR[0, rows, :].astype(jnp.float32)
        tg_ref[rows, :] = k * (total - I[rows, :].astype(jnp.float32))
    got("yfm0")
    got("yfp0")
    image_parts = both(YF, 0, ig_ref[...])
    got("xi")
    for h, part in enumerate(image_parts):
        rows = slice(h * H, (h + 1) * H)
        total = part + XR[1, rows, :].astype(jnp.float32)
        text = T[0, pl.ds(pl.multiple_of(own_rows + h * H, H), H), :]
        ig_ref[rows, :] = k * (total - text.astype(jnp.float32))
    for name in started:
        started[name].wait_send()


def per_device(image_codes, image_exps, text_codes, text_exps, logit_scale):
    R, D = image_codes.shape
    H = R // 2
    G = 4 * R
    RP = -(-R // 128) * 128
    bf16, f32 = jnp.bfloat16, jnp.float32
    vmem = pl.BlockSpec(memory_space=pltpu.VMEM)
    scratch = [
        pltpu.VMEM((4, G, D), bf16),
        pltpu.VMEM((8 * R, D), bf16),
        pltpu.VMEM((4, 8 * R, G), f32),
        pltpu.VMEM((4, 8 * R, G), bf16),
        pltpu.VMEM((8, RP, 128), f32),
        pltpu.VMEM((8, RP, 128), f32),
        pltpu.VMEM((4, 8, G), f32),
        pltpu.VMEM((4, 8, G), f32),
        pltpu.VMEM((8, RP, 128), f32),
        pltpu.VMEM((4, 8, G), f32),
        pltpu.VMEM((8, 8, RP), f32),
        pltpu.VMEM((16, 4, G), f32),
        pltpu.VMEM((8, 8, 128), f32),
        pltpu.VMEM((16, 8, 128), f32),
        pltpu.VMEM((4, 2, R, D), bf16),
        pltpu.VMEM((4, 2, R, D), bf16),
        pltpu.VMEM((3, 2, 2, H, D), bf16),
        pltpu.VMEM((2, 2, H, D), bf16),
        pltpu.VMEM((2, 2, 2, H, D), bf16),
        pltpu.VMEM((3, 2, 2, H, D), bf16),
        pltpu.VMEM((2, 2, H, D), bf16),
        pltpu.VMEM((2, 2, 2, H, D), bf16),
        pltpu.VMEM((2, R, D), bf16),
        pltpu.VMEM((2, R, D), bf16),
        pltpu.VMEM((RP, 128), f32),
        pltpu.SemaphoreType.DMA((len(MESSAGES),)),
        pltpu.SemaphoreType.DMA((len(MESSAGES),)),
    ]
    loss, image_grad, text_grad = pl.pallas_call(
        kernel,
        out_shape=[
            jax.ShapeDtypeStruct((8, 128), f32),
            jax.ShapeDtypeStruct((R, D), f32),
            jax.ShapeDtypeStruct((R, D), f32),
        ],
        in_specs=[vmem, vmem, vmem, vmem, pl.BlockSpec(memory_space=pltpu.SMEM)],
        out_specs=[vmem, vmem, vmem],
        scratch_shapes=scratch,
        compiler_params=pltpu.CompilerParams(
            collective_id=0, has_side_effects=True, vmem_limit_bytes=63 * 1024 * 1024
        ),
    )(image_codes, image_exps, text_codes, text_exps, logit_scale)
    return loss[0, 0], image_grad, text_grad


def solution(mesh):
    rows = P(("outer", "inner"), None)
    return jax.shard_map(
        per_device, mesh=mesh, in_specs=(rows, rows, rows, rows, P()), out_specs=(P(), rows, rows), check_vma=False
    )
```

```python
import functools

import jax
import jax.numpy as jnp
from jax import lax
from jax.experimental import pallas as pl
from jax.experimental.pallas import tpu as pltpu
from jax.sharding import PartitionSpec as P

LOG2E = 1.4426950408889634
LN2 = 0.6931471805599453
UNIT = 2.0 ** -17
LOW = -1e30
Z_OFF = (0, 1, 3, 2)
GROUP = {off: g for g, off in enumerate(Z_OFF)}
SLOTS = ((0, 0), (0, 1), (0, 3), (0, 2), (1, 0), (1, 1), (1, 3), (1, 2))
SLOT = {pos: s for s, pos in enumerate(SLOTS)}
INNER = [(r, a, b) for r in range(4) for a in range(2) for b in range(2)]
MESH = pl.DeviceIdType.MESH
MESSAGES = (
    [f"{n}{h}" for n in ("tx", "ix", "xs", "xi") for h in range(2)]
    + [f"tc{r}{a}" for r in range(4) for a in range(2)]
    + [f"{n}{d}{a}{h}" for n in ("tz", "iy", "zn", "yn") for d in "pm" for a in range(2) for h in range(2)]
    + [f"{n}{d}{a}" for n in ("th", "ih", "zh", "yh") for d in "pm" for a in range(2)]
    + [f"cs{a}{g}" for a in range(2) for g in range(4)]
    + [f"{n}{s}" for n in ("lr", "lo") for s in range(1, 8)]
    + [f"{n}{q}" for n in ("lc", "li") for q in range(1, 16)]
)
SEM = {name: i for i, name in enumerate(MESSAGES)}


def dot_nt(a, b):
    return lax.dot_general(a, b, (((1,), (1,)), ((), ())), preferred_element_type=jnp.float32)


def dot_nn(a, b):
    return jnp.dot(a, b, preferred_element_type=jnp.float32)


def dot_tn(a, b):
    return lax.dot_general(a, b, (((0,), (0,)), ((), ())), preferred_element_type=jnp.float32)


def kernel(
    ic_ref, ie_ref, tc_ref, te_ref, scale_ref, loss_ref, ig_ref, tg_ref,
    T, I, S, W, mr, sr, mc, sc, lcol, LR, LC, LO, LI,
    PT, CR, ZS, ZH, ZN, YS, YH, YN, XS, XR, dsum, exps, send_sems, recv_sems,
):
    R, D = ic_ref.shape
    H = R // 2
    Q = 2 * R
    C = 8 * R
    RP = LR.shape[2]
    ND = D // 128
    NB = ie_ref.shape[0]

    outer = lax.axis_index("outer")
    inner = lax.axis_index("inner")
    xh, y = outer // 4, outer % 4
    z, xl, c = inner // 4, (inner // 2) % 2, inner % 2

    def at(dh=0, dy=0, dz=0, dl=0, dc=0):
        h = xh if dh == 0 else 1 - xh
        l = xl if dl == 0 else 1 - xl
        k = c if dc == 0 else 1 - c
        return (h * 4 + (y + dy) % 4, ((z + dz) % 4) * 4 + l * 2 + k)

    outer_peers = [(s, SLOTS[s]) for s in range(1, 8)]
    inner_peers = [(q, INNER[q]) for q in range(1, 16)]
    barrier = pltpu.get_barrier_semaphore()
    for _, (a, r) in outer_peers:
        pl.semaphore_signal(barrier, inc=1, device_id=at(dh=a, dy=r), device_id_type=MESH)
    for _, (r, a, b) in inner_peers:
        pl.semaphore_signal(barrier, inc=1, device_id=at(dz=r, dl=a, dc=b), device_id_type=MESH)

    started = {}

    def send(name, src, dst, device):
        started[name] = pltpu.make_async_remote_copy(
            src_ref=src, dst_ref=dst, send_sem=send_sems.at[SEM[name]], recv_sem=recv_sems.at[SEM[name]],
            device_id=device, device_id_type=MESH,
        )
        started[name].start()

    def got(*names):
        for name in names:
            started[name].wait_recv()

    def core_row(b):
        return pl.multiple_of((c if b == 0 else 1 - c) * R, R)

    def trows(r, b, h=None):
        first = GROUP[r] * Q + core_row(b)
        if h is None:
            return pl.ds(pl.multiple_of(first, R), R)
        return pl.ds(pl.multiple_of(first + h * H, H), H)

    def tpart(a, r, h=None):
        return T.at[a, trows(r, 0, h), :]

    def ipart(a, r, h):
        return I.at[pl.ds(SLOT[a, r] * R + h * H, H), :]

    def columns(exps_ref):
        exps[0:NB, 0:R] = exps_ref[...]
        return exps[...].T

    def decode(codes_ref, exps_by_row, f):
        codes = codes_ref[:, f * 128 : (f + 1) * 128]
        field = (codes >> 3) & 15
        mantissa = codes & 7
        significand = jnp.where(field > 0, mantissa + 8, mantissa)
        shift = jnp.maximum(field, 1) - 1 + (exps_by_row[0:R, f : f + 1] + 8)
        magnitude = (significand << shift).astype(jnp.float32) * UNIT
        return jnp.where(codes > 127, -magnitude, magnitude)

    exps[...] = jnp.zeros(exps.shape, jnp.int32)
    image_exps = columns(ie_ref)
    text_exps = columns(te_ref)
    diag = jnp.zeros((R, 128), jnp.float32)
    for f in range(ND):
        image = decode(ic_ref, image_exps, f)
        text = decode(tc_ref, text_exps, f)
        diag = diag + image * text
        I[0:R, f * 128 : (f + 1) * 128] = image.astype(jnp.bfloat16)
        T[0, trows(0, 0), f * 128 : (f + 1) * 128] = text.astype(jnp.bfloat16)

    pl.semaphore_wait(barrier, 22)

    def ring_t(a, d, h):
        far = 1 if d == "m" else 3
        send(f"tz{d}{a}{h}", tpart(a, 0, h), tpart(a, -far % 4, h), at(dz=far))

    def ring_i(a, d, h):
        far = 1 if d == "m" else 3
        send(f"iy{d}{a}{h}", ipart(a, 0, h), ipart(a, -far % 4, h), at(dy=far))

    def on_t(a, d):
        far, h = (1, 0) if d == "m" else (3, 1)
        got(f"tz{d}{a}{h}")
        send(f"th{d}{a}", tpart(a, -far % 4, h), tpart(a, 2, h), at(dz=far))

    def on_i(a, d):
        far, h = (1, 0) if d == "m" else (3, 1)
        got(f"iy{d}{a}{h}")
        send(f"ih{d}{a}", ipart(a, -far % 4, h), ipart(a, 2, h), at(dy=far))

    def to_core(r, a):
        send(f"tc{r}{a}", tpart(a, r), tpart(a, r), at(dc=1))

    for d in "mp":
        ring_t(0, d, 0 if d == "m" else 1)
        ring_i(0, d, 0 if d == "m" else 1)
    for h in range(2):
        send(f"tx{h}", tpart(0, 0, h), tpart(1, 0, h), at(dl=1))
    for d in "mp":
        ring_t(0, d, 1 if d == "m" else 0)
        ring_i(0, d, 1 if d == "m" else 0)
    for h in range(2):
        send(f"ix{h}", ipart(0, 0, h), ipart(1, 0, h), at(dh=1))
    to_core(0, 0)

    dsum[0:R, :] = diag
    if RP > R:
        dsum[R:RP, :] = jnp.zeros((RP - R, 128), jnp.float32)
        for s in range(8):
            mr[s, R:RP, :] = jnp.zeros((RP - R, 128), jnp.float32)
            sr[s, R:RP, :] = jnp.ones((RP - R, 128), jnp.float32)
    for s in range(8):
        mr[s, 0:R, :] = jnp.full((R, 128), LOW, jnp.float32)
        sr[s, 0:R, :] = jnp.zeros((R, 128), jnp.float32)
    mc[...] = jnp.full(mc.shape, LOW, jnp.float32)
    sc[...] = jnp.zeros(sc.shape, jnp.float32)
    k = scale_ref[0]
    k2 = k * LOG2E

    def s_tile(a, lo, hi, first, last):
        rows, cols = slice(lo * R, hi * R), slice(first * Q, last * Q)
        tile = dot_nt(I[rows, :], T[a, cols, :]) * k2
        S[a, rows, cols] = tile
        parts = [tile[:, j : j + 128].reshape(hi - lo, R, 128) for j in range(0, (last - first) * Q, 128)]
        old = mr[lo:hi, 0:R, :]
        top = functools.reduce(jnp.maximum, parts, old)
        total = sr[lo:hi, 0:R, :] * jnp.exp2(old - top)
        for part in parts:
            total = total + jnp.exp2(part - top)
        mr[lo:hi, 0:R, :] = top
        sr[lo:hi, 0:R, :] = total
        by_col = tile.reshape((hi - lo) * R // 8, 8, (last - first) * Q)
        old = mc[a, :, cols]
        top = jnp.maximum(old, jnp.max(by_col, axis=0))
        sc[a, :, cols] = sc[a, :, cols] * jnp.exp2(old - top) + jnp.sum(jnp.exp2(by_col - top[None]), axis=0)
        mc[a, :, cols] = top

    on_t(0, "m")
    on_t(0, "p")
    on_i(0, "m")
    on_i(0, "p")
    got("tx0")
    ring_t(1, "m", 0)
    got("tx1")
    ring_t(1, "p", 1)
    ring_t(1, "m", 1)
    ring_t(1, "p", 0)
    to_core(0, 1)
    got("tzm01")
    to_core(3, 0)
    got("tzp00")
    to_core(1, 0)
    got("iym01", "iyp00", "tc00", "tc30", "tc10")
    s_tile(0, 0, 3, 0, 2)
    s_tile(0, 0, 3, 2, 3)
    got("thm0", "thp0")
    to_core(2, 0)
    got("ihm0", "ihp0", "ix0")
    ring_i(1, "m", 0)
    ring_i(1, "p", 0)
    s_tile(0, 3, 4, 0, 3)
    got("tc01")
    s_tile(1, 0, 4, 0, 1)
    got("ix1")
    ring_i(1, "m", 1)
    ring_i(1, "p", 1)
    on_t(1, "m")
    on_t(1, "p")
    got("tc20")
    s_tile(0, 0, 4, 3, 4)
    s_tile(0, 4, 5, 0, 4)
    got("tzm11")
    to_core(3, 1)
    got("tzp10")
    to_core(1, 1)
    on_i(1, "m")
    s_tile(1, 4, 5, 0, 1)
    got("tc31", "tc11")
    s_tile(1, 0, 5, 1, 3)
    on_i(1, "p")
    got("thm1", "thp1")
    to_core(2, 1)
    got("iym11", "iyp10")
    s_tile(0, 5, 7, 0, 2)
    s_tile(0, 5, 7, 2, 4)
    s_tile(1, 5, 7, 0, 3)
    got("tc21")
    s_tile(1, 0, 4, 3, 4)
    s_tile(1, 4, 7, 3, 4)
    got("ihm1", "ihp1")
    s_tile(0, 7, 8, 0, 4)
    s_tile(1, 7, 8, 0, 4)

    for a in range(2):
        m = mc[a]
        top = jnp.max(m, axis=0, keepdims=True)
        total = jnp.sum(sc[a] * jnp.exp2(m - top), axis=0, keepdims=True)
        LC[0, a : a + 1, :] = top + jnp.log(total) * LOG2E
    for q, (r, a, b) in inner_peers:
        send(f"lc{q}", LC.at[0], LC.at[INNER.index((-r % 4, a, b))], at(dz=r, dl=a, dc=b))
    for s in range(8):
        m = mr[s].T
        top = jnp.max(m, axis=0, keepdims=True)
        total = jnp.sum(sr[s].T * jnp.exp2(m - top), axis=0, keepdims=True)
        LR[0, s : s + 1, :] = top + jnp.log(total) * LOG2E
    for s, (a, r) in outer_peers:
        send(f"lr{s}", LR.at[0], LR.at[SLOT[a, -r % 4]], at(dh=a, dy=r))

    def merge(parts):
        top = functools.reduce(jnp.maximum, parts)
        total = functools.reduce(jnp.add, [jnp.exp2(part - top) for part in parts])
        return top + jnp.log(total) * LOG2E

    got(*[f"lc{q}" for q, _ in inner_peers])
    col_own = None
    for a in range(2):
        for g, r in enumerate(Z_OFF):
            parts = []
            for q, (dr, da, _) in enumerate(INNER):
                there = GROUP[(r - dr) % 4]
                parts.append(LC[q, (a ^ da) : (a ^ da) + 1, there * Q : (there + 1) * Q])
            lse = merge(parts)
            if a == 0 and g == 0:
                col_own = lse
            lcol[a, :, g * Q : (g + 1) * Q] = jnp.broadcast_to(lse + 1.0, (8, Q))
    got(*[f"lr{s}" for s, _ in outer_peers])
    row_own = None
    for s, (a, r) in enumerate(SLOTS):
        parts = []
        for p, (da, dr) in enumerate(SLOTS):
            there = SLOT[a ^ da, (r - dr) % 4]
            parts.append(LR[p, there : there + 1, :])
        lse = merge(parts)
        if s == 0:
            row_own = lse
        mr[s] = jnp.broadcast_to(lse + 1.0, (128, RP)).T

    def w_unit(a, first, last, slot):
        rows = pl.ds(pl.multiple_of(slot * R, R), R)
        by_row = mr[slot, 0:R, :]
        for j in range(first * Q, last * Q, 128):
            cols = slice(j, j + 128)
            s = S[a, rows, cols]
            w = jnp.exp2(s - by_row) + jnp.exp2(s - lcol[a, 0:1, cols])
            W[a, rows, cols] = w.astype(jnp.bfloat16)

    done = set()

    def w_need(a, first, last, slots):
        todo = [s for s in slots if (a, first, s) not in done]
        done.update((a, g, s) for g in range(first, last) for s in todo)
        while todo:
            lo = hi = todo.pop(0)
            while todo and todo[0] == hi + 1:
                hi = todo.pop(0)
            lax.fori_loop(lo, hi + 1, lambda slot, _: (w_unit(a, first, last, slot), 0)[1], 0)

    def t_terms(a, g):
        w_need(a, g, g + 1, range(8))
        if a == 0:
            started[f"cs1{g}"].wait_send()
        PT[g] = dot_tn(W[a, :, g * Q : (g + 1) * Q], I[...])
        send(f"cs{a}{g}", PT.at[g, pl.ds(core_row(1), R), :], CR.at[a, g], at(dc=1))

    def t_sum(a, g, h):
        rows = pl.ds(pl.multiple_of(core_row(0) + h * H, H), H)
        return PT[g, rows, :] + CR[a, g, h * H : (h + 1) * H, :]

    def i_terms(slot):
        for a in range(2):
            for g in range(4):
                w_need(a, g, g + 1, [slot])
        rows = slice(slot * R, (slot + 1) * R)
        return dot_nn(W[0, rows, :], T[0]) + dot_nn(W[1, rows, :], T[1])

    def far_t(a):
        got(f"cs{a}3")
        for i, d in enumerate("mp"):
            ZS[a, 0, i] = t_sum(a, 3, i).astype(jnp.bfloat16)
            send(f"zh{d}{a}", ZS.at[a, 0, i], ZH.at[a, i], at(dz=1 if d == "m" else 3))

    def far_i(a):
        term = i_terms(SLOT[a, 2])
        for i, d in enumerate("mp"):
            YS[a, 0, i] = term[i * H : (i + 1) * H].astype(jnp.bfloat16)
            send(f"yh{d}{a}", YS.at[a, 0, i], YH.at[a, i], at(dy=1 if d == "m" else 3))

    def near_t(a, d):
        i = "mp".index(d)
        g = GROUP[1 if d == "m" else 3]
        got(f"cs{a}{g}")
        for h in (1 - i, i):
            part = t_sum(a, g, h)
            if h == i:
                got(f"zh{d}{a}")
                part = part + ZH[a, i].astype(jnp.float32)
            ZS[a, 1 + i, h] = part.astype(jnp.bfloat16)
            send(f"zn{d}{a}{h}", ZS.at[a, 1 + i, h], ZN.at[a, i, h], at(dz=1 if d == "m" else 3))

    def near_i(a, d):
        i = "mp".index(d)
        term = i_terms(SLOT[a, 1 if d == "m" else 3])
        for h in (1 - i, i):
            part = term[h * H : (h + 1) * H]
            if h == i:
                got(f"yh{d}{a}")
                part = part + YH[a, i].astype(jnp.float32)
            YS[a, 1 + i, h] = part.astype(jnp.bfloat16)
            send(f"yn{d}{a}{h}", YS.at[a, 1 + i, h], YN.at[a, i, h], at(dy=1 if d == "m" else 3))

    def ring_sum(name, held, a, h, term):
        got(f"{name}m{a}{h}", f"{name}p{a}{h}")
        return term + (held[a, 0, h].astype(jnp.float32) + held[a, 1, h].astype(jnp.float32))

    t_terms(1, 3)
    far_i(1)
    t_terms(1, 1)
    far_t(1)
    t_terms(1, 2)
    near_t(1, "m")
    near_i(1, "m")
    near_t(1, "p")
    near_i(1, "p")
    t_terms(1, 0)
    ig_ref[...] = i_terms(SLOT[1, 0])
    got("cs10")
    for h in range(2):
        rows = slice(h * H, (h + 1) * H)
        tg_ref[rows, :] = t_sum(1, 0, h)
    t_terms(0, 3)
    far_i(0)
    t_terms(0, 1)
    far_t(0)
    for h in range(2):
        rows = slice(h * H, (h + 1) * H)
        XS[0, rows, :] = ring_sum("zn", ZN, 1, h, tg_ref[rows, :]).astype(jnp.bfloat16)
        send(f"xs{h}", XS.at[0, rows, :], XR.at[0, rows, :], at(dl=1))
    t_terms(0, 2)
    near_t(0, "m")
    near_i(0, "m")
    for h in range(2):
        rows = slice(h * H, (h + 1) * H)
        XS[1, rows, :] = ring_sum("yn", YN, 1, h, ig_ref[rows, :]).astype(jnp.bfloat16)
        send(f"xi{h}", XS.at[1, rows, :], XR.at[1, rows, :], at(dh=1))
    near_t(0, "p")
    near_i(0, "p")

    col_mine = jnp.where(c == 0, col_own[:, 0:R], col_own[:, R:Q])
    diag_own = jnp.sum(dsum[...].T, axis=0, keepdims=True)[:, 0:R] * k2
    LO[0] = jnp.full((8, 128), jnp.sum(row_own[:, 0:R] + col_mine - 2.0 * diag_own), jnp.float32)
    for s, (a, r) in outer_peers:
        send(f"lo{s}", LO.at[0], LO.at[SLOT[a, -r % 4]], at(dh=a, dy=r))

    t_terms(0, 0)

    def ring(values):
        return (values[0] + values[2]) + (values[1] + values[3])

    got(*[f"lo{s}" for s, _ in outer_peers])
    LI[0] = ring([LO[SLOT[0, r]] for r in range(4)]) + ring([LO[SLOT[1, r]] for r in range(4)])
    for q, (r, a, b) in inner_peers:
        send(f"li{q}", LI.at[0], LI.at[INNER.index((-r % 4, a, b))], at(dz=r, dl=a, dc=b))

    ig_ref[...] = i_terms(SLOT[0, 0])
    got("cs00")
    for h in range(2):
        rows = slice(h * H, (h + 1) * H)
        tg_ref[rows, :] = ring_sum("zn", ZN, 0, h, t_sum(0, 0, h)) - I[rows, :].astype(jnp.float32)
        text = T[0, trows(0, 0, h), :].astype(jnp.float32)
        ig_ref[rows, :] = ring_sum("yn", YN, 0, h, ig_ref[rows, :]) - text

    got(*[f"li{q}" for q, _ in inner_peers])
    by_z = []
    for r in range(4):
        v = [[LI[INNER.index((r, a, b))] for b in range(2)] for a in range(2)]
        by_z.append((v[0][0] + v[0][1]) + (v[1][0] + v[1][1]))
    loss_ref[...] = (ring(by_z) * (LN2 / (2 * 128 * R)))[0:1, 0:1]

    for h in range(2):
        rows = slice(h * H, (h + 1) * H)
        got(f"xs{h}")
        tg_ref[rows, :] = k * (tg_ref[rows, :] + XR[0, rows, :].astype(jnp.float32))
        got(f"xi{h}")
        ig_ref[rows, :] = k * (ig_ref[rows, :] + XR[1, rows, :].astype(jnp.float32))
    for name in started:
        if not name.startswith("cs1"):
            started[name].wait_send()


def per_device(image_codes, image_exps, text_codes, text_exps, logit_scale):
    R, D = image_codes.shape
    H = R // 2
    C = 8 * R
    RP = -(-R // 128) * 128
    bf16, f32 = jnp.bfloat16, jnp.float32
    vmem = pl.BlockSpec(memory_space=pltpu.VMEM)
    scratch = [
        pltpu.VMEM((2, C, D), bf16),
        pltpu.VMEM((C, D), bf16),
        pltpu.VMEM((2, C, C), f32),
        pltpu.VMEM((2, C, C), bf16),
        pltpu.VMEM((8, RP, 128), f32),
        pltpu.VMEM((8, RP, 128), f32),
        pltpu.VMEM((2, 8, C), f32),
        pltpu.VMEM((2, 8, C), f32),
        pltpu.VMEM((2, 8, C), f32),
        pltpu.VMEM((8, 8, RP), f32),
        pltpu.VMEM((16, 2, C), f32),
        pltpu.VMEM((8, 8, 128), f32),
        pltpu.VMEM((16, 8, 128), f32),
        pltpu.VMEM((4, 2 * R, D), f32),
        pltpu.VMEM((2, 4, R, D), f32),
        pltpu.VMEM((2, 3, 2, H, D), bf16),
        pltpu.VMEM((2, 2, H, D), bf16),
        pltpu.VMEM((2, 2, 2, H, D), bf16),
        pltpu.VMEM((2, 3, 2, H, D), bf16),
        pltpu.VMEM((2, 2, H, D), bf16),
        pltpu.VMEM((2, 2, 2, H, D), bf16),
        pltpu.VMEM((2, R, D), bf16),
        pltpu.VMEM((2, R, D), bf16),
        pltpu.VMEM((RP, 128), f32),
        pltpu.VMEM((128, RP), jnp.int32),
        pltpu.SemaphoreType.DMA((len(MESSAGES),)),
        pltpu.SemaphoreType.DMA((len(MESSAGES),)),
    ]
    loss, image_grad, text_grad = pl.pallas_call(
        kernel,
        out_shape=[
            jax.ShapeDtypeStruct((1, 1), f32),
            jax.ShapeDtypeStruct((R, D), f32),
            jax.ShapeDtypeStruct((R, D), f32),
        ],
        in_specs=[vmem, vmem, vmem, vmem, pl.BlockSpec(memory_space=pltpu.SMEM)],
        out_specs=[vmem, vmem, vmem],
        scratch_shapes=scratch,
        compiler_params=pltpu.CompilerParams(
            collective_id=0, has_side_effects=True, vmem_limit_bytes=63 * 1024 * 1024
        ),
    )(image_codes, image_exps.T, text_codes, text_exps.T, logit_scale)
    return loss.reshape(()), image_grad, text_grad


def solution(mesh):
    rows = P(("outer", "inner"), None)
    return jax.shard_map(
        per_device, mesh=mesh, in_specs=(rows, rows, rows, rows, P()), out_specs=(P(), rows, rows), check_vma=False
    )
```

```python
import functools

import jax
import jax.numpy as jnp
from jax import lax
from jax.experimental import pallas as pl
from jax.experimental.pallas import tpu as pltpu
from jax.sharding import PartitionSpec as P

LOG2E = 1.4426950408889634
LN2 = 0.6931471805599453
UNIT = 2.0 ** -17
LOW = -1e30
Z_OFF = (0, 1, 3, 2)
GROUP = {off: g for g, off in enumerate(Z_OFF)}
SLOTS = ((0, 0), (0, 1), (0, 3), (0, 2), (1, 0), (1, 1), (1, 3), (1, 2))
SLOT = {pos: s for s, pos in enumerate(SLOTS)}
INNER = [(r, a, b) for r in range(4) for a in range(2) for b in range(2)]
MESH = pl.DeviceIdType.MESH
MESSAGES = (
    [f"{n}{h}" for n in ("tx", "ix", "xs", "xi") for h in range(2)]
    + [f"tc{r}{a}" for r in range(4) for a in range(2)]
    + [f"{n}{d}{a}{h}" for n in ("tz", "iy", "zn", "yn") for d in "pm" for a in range(2) for h in range(2)]
    + [f"{n}{d}{a}" for n in ("th", "ih", "zh", "yh") for d in "pm" for a in range(2)]
    + [f"cs{a}{g}" for a in range(2) for g in range(4)]
    + [f"{n}{s}" for n in ("lr", "lo") for s in range(1, 8)]
    + [f"{n}{q}" for n in ("lc", "li") for q in range(1, 16)]
)
SEM = {name: i for i, name in enumerate(MESSAGES)}


def dot_nt(a, b):
    return lax.dot_general(a, b, (((1,), (1,)), ((), ())), preferred_element_type=jnp.float32)


def dot_nn(a, b):
    return jnp.dot(a, b, preferred_element_type=jnp.float32)


def dot_tn(a, b):
    return lax.dot_general(a, b, (((0,), (0,)), ((), ())), preferred_element_type=jnp.float32)


def kernel(
    ic_ref, ie_ref, tc_ref, te_ref, scale_ref, loss_ref, ig_ref, tg_ref,
    T, I, S, W, mr, sr, mc, sc, lcol, LR, LC, LO, LI,
    PT, CR, ZS, ZH, ZN, YS, YH, YN, KI, XS, XR, dsum, exps, send_sems, recv_sems,
):
    R, D = ic_ref.shape
    H = R // 2
    Q = 2 * R
    C = 8 * R
    RP = LR.shape[2]
    ND = D // 128
    NB = ie_ref.shape[0]

    outer = lax.axis_index("outer")
    inner = lax.axis_index("inner")
    xh, y = outer // 4, outer % 4
    z, xl, c = inner // 4, (inner // 2) % 2, inner % 2

    def at(dh=0, dy=0, dz=0, dl=0, dc=0):
        h = xh if dh == 0 else 1 - xh
        l = xl if dl == 0 else 1 - xl
        k = c if dc == 0 else 1 - c
        return (h * 4 + (y + dy) % 4, ((z + dz) % 4) * 4 + l * 2 + k)

    outer_peers = [(s, SLOTS[s]) for s in range(1, 8)]
    inner_peers = [(q, INNER[q]) for q in range(1, 16)]
    barrier = pltpu.get_barrier_semaphore()
    for _, (a, r) in outer_peers:
        pl.semaphore_signal(barrier, inc=1, device_id=at(dh=a, dy=r), device_id_type=MESH)
    for _, (r, a, b) in inner_peers:
        pl.semaphore_signal(barrier, inc=1, device_id=at(dz=r, dl=a, dc=b), device_id_type=MESH)

    started = {}

    def send(name, src, dst, device):
        started[name] = pltpu.make_async_remote_copy(
            src_ref=src, dst_ref=dst, send_sem=send_sems.at[SEM[name]], recv_sem=recv_sems.at[SEM[name]],
            device_id=device, device_id_type=MESH,
        )
        started[name].start()

    def got(*names):
        for name in names:
            started[name].wait_recv()

    def core_row(b):
        return pl.multiple_of((c if b == 0 else 1 - c) * R, R)

    def trows(r, b, h=None):
        first = GROUP[r] * Q + core_row(b)
        if h is None:
            return pl.ds(pl.multiple_of(first, R), R)
        return pl.ds(pl.multiple_of(first + h * H, H), H)

    def tpart(a, r, h=None):
        return T.at[a, trows(r, 0, h), :]

    def ipart(a, r, h):
        return I.at[pl.ds(SLOT[a, r] * R + h * H, H), :]

    def columns(exps_ref):
        exps[0:NB, 0:R] = exps_ref[...]
        return exps[...].T

    def decode(codes_ref, exps_by_row, f):
        codes = codes_ref[:, f * 128 : (f + 1) * 128]
        field = (codes >> 3) & 15
        mantissa = codes & 7
        significand = jnp.where(field > 0, mantissa + 8, mantissa)
        shift = jnp.maximum(field, 1) - 1 + (exps_by_row[0:R, f : f + 1] + 8)
        magnitude = (significand << shift).astype(jnp.float32) * UNIT
        return jnp.where(codes > 127, -magnitude, magnitude)

    exps[...] = jnp.zeros(exps.shape, jnp.int32)
    image_exps = columns(ie_ref)
    text_exps = columns(te_ref)
    diag = jnp.zeros((R, 128), jnp.float32)
    for f in range(ND):
        image = decode(ic_ref, image_exps, f)
        text = decode(tc_ref, text_exps, f)
        diag = diag + image * text
        I[0:R, f * 128 : (f + 1) * 128] = image.astype(jnp.bfloat16)
        T[0, trows(0, 0), f * 128 : (f + 1) * 128] = text.astype(jnp.bfloat16)

    pl.semaphore_wait(barrier, 22)

    def ring_t(a, d, h):
        far = 1 if d == "m" else 3
        send(f"tz{d}{a}{h}", tpart(a, 0, h), tpart(a, -far % 4, h), at(dz=far))

    def ring_i(a, d, h):
        far = 1 if d == "m" else 3
        send(f"iy{d}{a}{h}", ipart(a, 0, h), ipart(a, -far % 4, h), at(dy=far))

    def on_t(a, d):
        far, h = (1, 0) if d == "m" else (3, 1)
        got(f"tz{d}{a}{h}")
        send(f"th{d}{a}", tpart(a, -far % 4, h), tpart(a, 2, h), at(dz=far))

    def on_i(a, d):
        far, h = (1, 0) if d == "m" else (3, 1)
        got(f"iy{d}{a}{h}")
        send(f"ih{d}{a}", ipart(a, -far % 4, h), ipart(a, 2, h), at(dy=far))

    def to_core(r, a):
        send(f"tc{r}{a}", tpart(a, r), tpart(a, r), at(dc=1))

    for d in "mp":
        ring_t(0, d, 0 if d == "m" else 1)
        ring_i(0, d, 0 if d == "m" else 1)
    for h in range(2):
        send(f"tx{h}", tpart(0, 0, h), tpart(1, 0, h), at(dl=1))
    for d in "mp":
        ring_t(0, d, 1 if d == "m" else 0)
        ring_i(0, d, 1 if d == "m" else 0)
    for h in range(2):
        send(f"ix{h}", ipart(0, 0, h), ipart(1, 0, h), at(dh=1))
    to_core(0, 0)

    dsum[0:R, :] = diag
    if RP > R:
        dsum[R:RP, :] = jnp.zeros((RP - R, 128), jnp.float32)
        for s in range(8):
            mr[s, R:RP, :] = jnp.zeros((RP - R, 128), jnp.float32)
            sr[s, R:RP, :] = jnp.ones((RP - R, 128), jnp.float32)
    for s in range(8):
        mr[s, 0:R, :] = jnp.full((R, 128), LOW, jnp.float32)
        sr[s, 0:R, :] = jnp.zeros((R, 128), jnp.float32)
    mc[...] = jnp.full(mc.shape, LOW, jnp.float32)
    sc[...] = jnp.zeros(sc.shape, jnp.float32)
    k = scale_ref[0]
    k2 = k * LOG2E

    def s_tile(a, lo, hi, first, last):
        rows, cols = slice(lo * R, hi * R), slice(first * Q, last * Q)
        tile = dot_nt(I[rows, :], T[a, cols, :]) * k2
        S[a, rows, cols] = tile
        parts = [tile[:, j : j + 128].reshape(hi - lo, R, 128) for j in range(0, (last - first) * Q, 128)]
        old = mr[lo:hi, 0:R, :]
        top = functools.reduce(jnp.maximum, parts, old)
        total = sr[lo:hi, 0:R, :] * jnp.exp2(old - top)
        for part in parts:
            total = total + jnp.exp2(part - top)
        mr[lo:hi, 0:R, :] = top
        sr[lo:hi, 0:R, :] = total
        by_col = tile.reshape((hi - lo) * R // 8, 8, (last - first) * Q)
        old = mc[a, :, cols]
        top = jnp.maximum(old, jnp.max(by_col, axis=0))
        sc[a, :, cols] = sc[a, :, cols] * jnp.exp2(old - top) + jnp.sum(jnp.exp2(by_col - top[None]), axis=0)
        mc[a, :, cols] = top

    on_t(0, "m")
    on_t(0, "p")
    on_i(0, "m")
    on_i(0, "p")
    got("tx0")
    ring_t(1, "m", 0)
    got("tx1")
    ring_t(1, "p", 1)
    ring_t(1, "m", 1)
    ring_t(1, "p", 0)
    to_core(0, 1)
    got("tzm01")
    to_core(3, 0)
    got("tzp00")
    to_core(1, 0)
    got("iym01", "iyp00", "tc00", "tc30", "tc10")
    s_tile(0, 0, 3, 0, 2)
    s_tile(0, 0, 3, 2, 3)
    got("thm0", "thp0")
    to_core(2, 0)
    got("ihm0", "ihp0", "ix0")
    ring_i(1, "m", 0)
    ring_i(1, "p", 0)
    s_tile(0, 3, 4, 0, 3)
    got("tc01")
    s_tile(1, 0, 4, 0, 1)
    got("ix1")
    ring_i(1, "m", 1)
    ring_i(1, "p", 1)
    on_t(1, "m")
    on_t(1, "p")
    got("tc20")
    s_tile(0, 0, 4, 3, 4)
    s_tile(0, 4, 5, 0, 4)
    got("tzm11")
    to_core(3, 1)
    got("tzp10")
    to_core(1, 1)
    on_i(1, "m")
    s_tile(1, 4, 5, 0, 1)
    got("tc31", "tc11")
    s_tile(1, 0, 5, 1, 3)
    on_i(1, "p")
    got("thm1", "thp1")
    to_core(2, 1)
    got("iym11", "iyp10")
    s_tile(0, 5, 7, 0, 2)
    s_tile(0, 5, 7, 2, 4)
    s_tile(1, 5, 7, 0, 3)
    got("tc21")
    s_tile(1, 0, 4, 3, 4)
    s_tile(1, 4, 7, 3, 4)
    def row_lse(s):
        m = mr[s].T
        top = jnp.max(m, axis=0, keepdims=True)
        total = jnp.sum(sr[s].T * jnp.exp2(m - top), axis=0, keepdims=True)
        LR[0, s : s + 1, :] = top + jnp.log(total) * LOG2E

    for s in range(7):
        row_lse(s)
    got("ihm1", "ihp1")
    s_tile(0, 7, 8, 0, 4)
    s_tile(1, 7, 8, 0, 4)
    for a in range(2):
        m = mc[a]
        top = jnp.max(m, axis=0, keepdims=True)
        total = jnp.sum(sc[a] * jnp.exp2(m - top), axis=0, keepdims=True)
        LC[0, a : a + 1, :] = top + jnp.log(total) * LOG2E
    for q, (r, a, b) in inner_peers:
        send(f"lc{q}", LC.at[0], LC.at[INNER.index((-r % 4, a, b))], at(dz=r, dl=a, dc=b))
    row_lse(7)
    for s, (a, r) in outer_peers:
        send(f"lr{s}", LR.at[0], LR.at[SLOT[a, -r % 4]], at(dh=a, dy=r))

    def merge(parts):
        top = functools.reduce(jnp.maximum, parts)
        total = functools.reduce(jnp.add, [jnp.exp2(part - top) for part in parts])
        return top + jnp.log(total) * LOG2E

    got(*[f"lc{q}" for q, _ in inner_peers])
    col_own = None
    for a in range(2):
        for g, r in enumerate(Z_OFF):
            parts = []
            for q, (dr, da, _) in enumerate(INNER):
                there = GROUP[(r - dr) % 4]
                parts.append(LC[q, (a ^ da) : (a ^ da) + 1, there * Q : (there + 1) * Q])
            lse = merge(parts)
            if a == 0 and g == 0:
                col_own = lse
            lcol[a, :, g * Q : (g + 1) * Q] = jnp.broadcast_to(lse + 1.0, (8, Q))
    got(*[f"lr{s}" for s, _ in outer_peers])
    row_own = None
    for s, (a, r) in enumerate(SLOTS):
        parts = []
        for p, (da, dr) in enumerate(SLOTS):
            there = SLOT[a ^ da, (r - dr) % 4]
            parts.append(LR[p, there : there + 1, :])
        lse = merge(parts)
        if s == 0:
            row_own = lse
        mr[s] = jnp.broadcast_to(lse + 1.0, (128, RP)).T

    col_mine = jnp.where(c == 0, col_own[:, 0:R], col_own[:, R:Q])
    diag_own = jnp.sum(dsum[...].T, axis=0, keepdims=True)[:, 0:R] * k2
    LO[0] = jnp.full((1, 128), jnp.sum(row_own[:, 0:R] + col_mine - 2.0 * diag_own), jnp.float32)
    for s, (a, r) in outer_peers:
        send(f"lo{s}", LO.at[0], LO.at[SLOT[a, -r % 4]], at(dh=a, dy=r))

    def w_unit(a, g, slot):
        rows = slice(slot * R, (slot + 1) * R)
        by_row = mr[slot, 0:R, :]
        for j in range(g * Q, (g + 1) * Q, 128):
            cols = slice(j, j + 128)
            s = S[a, rows, cols]
            w = jnp.exp2(s - by_row) + jnp.exp2(s - lcol[a, 0:1, cols])
            W[a, rows, cols] = w.astype(jnp.bfloat16)

    done = set()

    def weights(needed):
        for unit in needed:
            if unit not in done:
                done.add(unit)
                w_unit(*unit)

    def for_t(a, g):
        return [(a, g, slot) for slot in range(8)]

    def for_i(slot):
        return [(a, g, slot) for a in range(2) for g in range(4)]

    def t_terms(a, g, then=()):
        weights(for_t(a, g))
        if a == 0:
            started[f"cs1{g}"].wait_send()
        weights(then)
        PT[g] = dot_tn(W[a, :, g * Q : (g + 1) * Q], I[...])
        send(f"cs{a}{g}", PT.at[g, pl.ds(core_row(1), R), :], CR.at[a, g], at(dc=1))

    def t_sum(a, g, h):
        rows = pl.ds(pl.multiple_of(core_row(0) + h * H, H), H)
        return PT[g, rows, :] + CR[a, g, h * H : (h + 1) * H, :]

    def i_terms(slot, then=()):
        weights(for_i(slot))
        weights(then)
        rows = slice(slot * R, (slot + 1) * R)
        return dot_nn(W[0, rows, :], T[0]) + dot_nn(W[1, rows, :], T[1])

    def far_t(a):
        got(f"cs{a}3")
        for i, d in enumerate("mp"):
            ZS[a, 0, i] = t_sum(a, 3, i).astype(jnp.bfloat16)
            send(f"zh{d}{a}", ZS.at[a, 0, i], ZH.at[a, i], at(dz=1 if d == "m" else 3))

    def far_i(a, then):
        term = i_terms(SLOT[a, 2], then)
        for i, d in enumerate("mp"):
            YS[a, 0, i] = term[i * H : (i + 1) * H].astype(jnp.bfloat16)
            send(f"yh{d}{a}", YS.at[a, 0, i], YH.at[a, i], at(dy=1 if d == "m" else 3))

    def z_send(a, i, h, part):
        ZS[a, 1 + i, h] = part.astype(jnp.bfloat16)
        send(f"zn{'mp'[i]}{a}{h}", ZS.at[a, 1 + i, h], ZN.at[a, i, h], at(dz=3 if i else 1))

    def y_send(a, i, h, part):
        YS[a, 1 + i, h] = part.astype(jnp.bfloat16)
        send(f"yn{'mp'[i]}{a}{h}", YS.at[a, 1 + i, h], YN.at[a, i, h], at(dy=3 if i else 1))

    def near_t(a, i):
        g = GROUP[3 if i else 1]
        if (a, i) != (1, 1):
            got(f"cs{a}{g}")
        z_send(a, i, 1 - i, t_sum(a, g, 1 - i))

    def near_t_met(a, i):
        g = GROUP[3 if i else 1]
        if (a, i) == (1, 1):
            got(f"cs{a}{g}")
        got(f"zh{'mp'[i]}{a}")
        z_send(a, i, i, t_sum(a, g, i) + ZH[a, i].astype(jnp.float32))

    def near_i(a, i, then):
        term = i_terms(SLOT[a, 3 if i else 1], then)
        y_send(a, i, 1 - i, term[(1 - i) * H : (2 - i) * H])
        KI[i] = term[i * H : (i + 1) * H]

    def near_i_met(a, i):
        got(f"yh{'mp'[i]}{a}")
        y_send(a, i, i, KI[i] + YH[a, i].astype(jnp.float32))

    def ring_sum(name, held, a, h, term):
        got(f"{name}m{a}{h}", f"{name}p{a}{h}")
        return term + (held[a, 0, h].astype(jnp.float32) + held[a, 1, h].astype(jnp.float32))

    halves = [(h, slice(h * H, (h + 1) * H)) for h in range(2)]
    t_terms(1, 3, for_t(1, 1))
    t_terms(1, 1, for_t(1, 2))
    far_t(1)
    t_terms(1, 2, for_i(SLOT[1, 2]))
    near_t(1, 0)
    far_i(1, for_t(1, 0))

    def ring(values):
        return (values[0] + values[2]) + (values[1] + values[3])

    got(*[f"lo{s}" for s, _ in outer_peers])
    LI[0] = ring([LO[SLOT[0, r]] for r in range(4)]) + ring([LO[SLOT[1, r]] for r in range(4)])
    for q, (r, a, b) in inner_peers:
        send(f"li{q}", LI.at[0], LI.at[INNER.index((-r % 4, a, b))], at(dz=r, dl=a, dc=b))

    t_terms(1, 0, for_i(SLOT[1, 1]))
    near_t_met(1, 1)
    near_t(1, 1)
    near_t_met(1, 0)
    near_i(1, 0, for_i(SLOT[1, 3]))
    near_i(1, 1, for_i(SLOT[1, 0]))
    near_i_met(1, 0)
    near_i_met(1, 1)
    ig_ref[...] = i_terms(SLOT[1, 0], for_t(0, 3))
    t_terms(0, 3, for_t(0, 1))

    def across_t(h):
        rows = halves[h][1]
        XS[0, rows, :] = ring_sum("zn", ZN, 1, h, t_sum(1, 0, h)).astype(jnp.bfloat16)
        send(f"xs{h}", XS.at[0, rows, :], XR.at[0, rows, :], at(dl=1))

    def across_i(h):
        rows = halves[h][1]
        XS[1, rows, :] = ring_sum("yn", YN, 1, h, ig_ref[rows, :]).astype(jnp.bfloat16)
        send(f"xi{h}", XS.at[1, rows, :], XR.at[1, rows, :], at(dh=1))

    got("cs10")
    across_t(1)
    t_terms(0, 1, for_t(0, 2))
    far_t(0)
    t_terms(0, 2, for_i(SLOT[0, 2]))
    across_t(0)
    far_i(0, for_i(SLOT[0, 1]))
    near_t(0, 0)
    near_t(0, 1)
    across_i(0)
    across_i(1)
    near_i(0, 0, for_i(SLOT[0, 3]))
    near_i(0, 1, for_t(0, 0))
    near_t_met(0, 0)
    near_t_met(0, 1)
    near_i_met(0, 0)
    near_i_met(0, 1)
    t_terms(0, 0, for_i(SLOT[0, 0]))
    ig_ref[...] = i_terms(SLOT[0, 0])
    got("cs00")
    for h, rows in halves:
        tg_ref[rows, :] = ring_sum("zn", ZN, 0, h, t_sum(0, 0, h)) - I[rows, :].astype(jnp.float32)
    for h, rows in halves:
        text = T[0, trows(0, 0, h), :].astype(jnp.float32)
        ig_ref[rows, :] = ring_sum("yn", YN, 0, h, ig_ref[rows, :]) - text

    got(*[f"li{q}" for q, _ in inner_peers])
    by_z = []
    for r in range(4):
        v = [[LI[INNER.index((r, a, b))] for b in range(2)] for a in range(2)]
        by_z.append((v[0][0] + v[0][1]) + (v[1][0] + v[1][1]))
    loss_ref[...] = (ring(by_z) * (LN2 / (2 * 128 * R)))[0:1, 0:1]

    for h in range(2):
        rows = slice(h * H, (h + 1) * H)
        got(f"xs{h}")
        tg_ref[rows, :] = k * (tg_ref[rows, :] + XR[0, rows, :].astype(jnp.float32))
        got(f"xi{h}")
        ig_ref[rows, :] = k * (ig_ref[rows, :] + XR[1, rows, :].astype(jnp.float32))
    for name in started:
        if not name.startswith("cs1"):
            started[name].wait_send()


def per_device(image_codes, image_exps, text_codes, text_exps, logit_scale):
    R, D = image_codes.shape
    H = R // 2
    C = 8 * R
    RP = -(-R // 128) * 128
    bf16, f32 = jnp.bfloat16, jnp.float32
    vmem = pl.BlockSpec(memory_space=pltpu.VMEM)
    scratch = [
        pltpu.VMEM((2, C, D), bf16),
        pltpu.VMEM((C, D), bf16),
        pltpu.VMEM((2, C, C), f32),
        pltpu.VMEM((2, C, C), bf16),
        pltpu.VMEM((8, RP, 128), f32),
        pltpu.VMEM((8, RP, 128), f32),
        pltpu.VMEM((2, 8, C), f32),
        pltpu.VMEM((2, 8, C), f32),
        pltpu.VMEM((2, 8, C), f32),
        pltpu.VMEM((8, 8, RP), f32),
        pltpu.VMEM((16, 2, C), f32),
        pltpu.VMEM((8, 1, 128), f32),
        pltpu.VMEM((16, 1, 128), f32),
        pltpu.VMEM((4, 2 * R, D), f32),
        pltpu.VMEM((2, 4, R, D), f32),
        pltpu.VMEM((2, 3, 2, H, D), bf16),
        pltpu.VMEM((2, 2, H, D), bf16),
        pltpu.VMEM((2, 2, 2, H, D), bf16),
        pltpu.VMEM((2, 3, 2, H, D), bf16),
        pltpu.VMEM((2, 2, H, D), bf16),
        pltpu.VMEM((2, 2, 2, H, D), bf16),
        pltpu.VMEM((2, H, D), f32),
        pltpu.VMEM((2, R, D), bf16),
        pltpu.VMEM((2, R, D), bf16),
        pltpu.VMEM((RP, 128), f32),
        pltpu.VMEM((128, RP), jnp.int32),
        pltpu.SemaphoreType.DMA((len(MESSAGES),)),
        pltpu.SemaphoreType.DMA((len(MESSAGES),)),
    ]
    loss, image_grad, text_grad = pl.pallas_call(
        kernel,
        out_shape=[
            jax.ShapeDtypeStruct((1, 1), f32),
            jax.ShapeDtypeStruct((R, D), f32),
            jax.ShapeDtypeStruct((R, D), f32),
        ],
        in_specs=[vmem, vmem, vmem, vmem, pl.BlockSpec(memory_space=pltpu.SMEM)],
        out_specs=[vmem, vmem, vmem],
        scratch_shapes=scratch,
        compiler_params=pltpu.CompilerParams(
            collective_id=0, has_side_effects=True, vmem_limit_bytes=63 * 1024 * 1024
        ),
    )(image_codes, image_exps.T, text_codes, text_exps.T, logit_scale)
    return loss.reshape(()), image_grad, text_grad


def solution(mesh):
    rows = P(("outer", "inner"), None)
    return jax.shard_map(
        per_device, mesh=mesh, in_specs=(rows, rows, rows, rows, P()), out_specs=(P(), rows, rows), check_vma=False
    )
```

```python
import functools

import jax
import jax.numpy as jnp
from jax import lax
from jax.experimental import pallas as pl
from jax.experimental.pallas import tpu as pltpu
from jax.sharding import PartitionSpec as P

LOG2E = 1.4426950408889634
LN2 = 0.6931471805599453
UNIT = 2.0 ** -17
LOW = -1e30
Z_OFF = (0, 1, 3, 2)
GROUP = {off: g for g, off in enumerate(Z_OFF)}
SLOTS = ((0, 0), (0, 1), (0, 3), (0, 2), (1, 0), (1, 1), (1, 3), (1, 2))
SLOT = {pos: s for s, pos in enumerate(SLOTS)}
INNER = [(r, a, b) for r in range(4) for a in range(2) for b in range(2)]
MESH = pl.DeviceIdType.MESH
MESSAGES = (
    [f"{n}{h}" for n in ("tx", "ix", "xs", "xi") for h in range(2)]
    + [f"tc{r}{a}" for r in range(4) for a in range(2)]
    + [f"{n}{d}{a}{h}" for n in ("tz", "iy", "zn", "yn") for d in "pm" for a in range(2) for h in range(2)]
    + [f"{n}{d}{a}" for n in ("th", "ih", "zh", "yh") for d in "pm" for a in range(2)]
    + [f"cs{a}{g}" for a in range(2) for g in range(4)]
    + [f"{n}{s}" for n in ("lr", "lo") for s in range(1, 8)]
    + [f"{n}{q}" for n in ("lc", "li") for q in range(1, 16)]
)
SEM = {name: i for i, name in enumerate(MESSAGES)}


def dot_nt(a, b):
    return lax.dot_general(a, b, (((1,), (1,)), ((), ())), preferred_element_type=jnp.float32)


def dot_nn(a, b):
    return jnp.dot(a, b, preferred_element_type=jnp.float32)


def dot_tn(a, b):
    return lax.dot_general(a, b, (((0,), (0,)), ((), ())), preferred_element_type=jnp.float32)


def kernel(
    ic_hbm, ie_ref, tc_hbm, te_ref, scale_ref, loss_ref, ig_hbm, tg_hbm,
    T, I, S, W, mr, sr, mc, sc, lcol, LR, LC, LO, LI,
    PT, CR, ZS, ZH, ZN, YS, YH, YN, KI, XS, XR, dsum, exps, codes, grads, own_sems, send_sems, recv_sems,
):
    R, D = ic_hbm.shape
    ic_ref, tc_ref = codes.at[0], codes.at[1]
    ig_ref, tg_ref = grads.at[0], grads.at[1]
    H = R // 2
    Q = 2 * R
    C = 8 * R
    RP = LR.shape[2]
    ND = D // 128
    NB = ie_ref.shape[0]

    outer = lax.axis_index("outer")
    inner = lax.axis_index("inner")
    xh, y = outer // 4, outer % 4
    z, xl, c = inner // 4, (inner // 2) % 2, inner % 2

    def at(dh=0, dy=0, dz=0, dl=0, dc=0):
        h = xh if dh == 0 else 1 - xh
        l = xl if dl == 0 else 1 - xl
        k = c if dc == 0 else 1 - c
        return (h * 4 + (y + dy) % 4, ((z + dz) % 4) * 4 + l * 2 + k)

    outer_peers = [(s, SLOTS[s]) for s in range(1, 8)]
    inner_peers = [(q, INNER[q]) for q in range(1, 16)]
    barrier = pltpu.get_barrier_semaphore()
    for _, (a, r) in outer_peers:
        pl.semaphore_signal(barrier, inc=1, device_id=at(dh=a, dy=r), device_id_type=MESH)
    for _, (r, a, b) in inner_peers:
        pl.semaphore_signal(barrier, inc=1, device_id=at(dz=r, dl=a, dc=b), device_id_type=MESH)
    text_in = pltpu.make_async_copy(tc_hbm, tc_ref, own_sems.at[0])
    image_in = pltpu.make_async_copy(ic_hbm, ic_ref, own_sems.at[1])
    text_in.start()
    image_in.start()

    started = {}

    def send(name, src, dst, device):
        started[name] = pltpu.make_async_remote_copy(
            src_ref=src, dst_ref=dst, send_sem=send_sems.at[SEM[name]], recv_sem=recv_sems.at[SEM[name]],
            device_id=device, device_id_type=MESH,
        )
        started[name].start()

    def got(*names):
        for name in names:
            started[name].wait_recv()

    def core_row(b):
        return pl.multiple_of((c if b == 0 else 1 - c) * R, R)

    def trows(r, b, h=None):
        first = GROUP[r] * Q + core_row(b)
        if h is None:
            return pl.ds(pl.multiple_of(first, R), R)
        return pl.ds(pl.multiple_of(first + h * H, H), H)

    def tpart(a, r, h=None):
        return T.at[a, trows(r, 0, h), :]

    def ipart(a, r, h):
        return I.at[pl.ds(SLOT[a, r] * R + h * H, H), :]

    def columns(exps_ref):
        exps[0:NB, 0:R] = exps_ref[...]
        return exps[...].T

    def decode(codes_ref, exps_by_row, f):
        codes = codes_ref[:, f * 128 : (f + 1) * 128]
        field = (codes >> 3) & 15
        mantissa = codes & 7
        significand = jnp.where(field > 0, mantissa + 8, mantissa)
        shift = jnp.maximum(field, 1) - 1 + (exps_by_row[0:R, f : f + 1] + 8)
        magnitude = (significand << shift).astype(jnp.float32) * UNIT
        return jnp.where(codes > 127, -magnitude, magnitude)

    exps[...] = jnp.zeros(exps.shape, jnp.int32)
    image_exps = columns(ie_ref)
    text_exps = columns(te_ref)
    text_in.wait()
    for f in range(ND):
        text = decode(tc_ref, text_exps, f)
        T[0, trows(0, 0), f * 128 : (f + 1) * 128] = text.astype(jnp.bfloat16)

    pl.semaphore_wait(barrier, 22)

    def ring_t(a, d, h):
        far = 1 if d == "m" else 3
        send(f"tz{d}{a}{h}", tpart(a, 0, h), tpart(a, -far % 4, h), at(dz=far))

    def ring_i(a, d, h):
        far = 1 if d == "m" else 3
        send(f"iy{d}{a}{h}", ipart(a, 0, h), ipart(a, -far % 4, h), at(dy=far))

    def on_t(a, d):
        far, h = (1, 0) if d == "m" else (3, 1)
        got(f"tz{d}{a}{h}")
        send(f"th{d}{a}", tpart(a, -far % 4, h), tpart(a, 2, h), at(dz=far))

    def on_i(a, d):
        far, h = (1, 0) if d == "m" else (3, 1)
        got(f"iy{d}{a}{h}")
        send(f"ih{d}{a}", ipart(a, -far % 4, h), ipart(a, 2, h), at(dy=far))

    def to_core(r, a):
        send(f"tc{r}{a}", tpart(a, r), tpart(a, r), at(dc=1))

    ring_t(0, "m", 0)
    ring_t(0, "p", 1)
    for h in range(2):
        send(f"tx{h}", tpart(0, 0, h), tpart(1, 0, h), at(dl=1))
    ring_t(0, "m", 1)
    ring_t(0, "p", 0)
    to_core(0, 0)
    image_in.wait()
    diag = jnp.zeros((R, 128), jnp.float32)
    for f in range(ND):
        image = decode(ic_ref, image_exps, f)
        diag = diag + image * T[0, trows(0, 0), f * 128 : (f + 1) * 128].astype(jnp.float32)
        I[0:R, f * 128 : (f + 1) * 128] = image.astype(jnp.bfloat16)
    ring_i(0, "m", 0)
    ring_i(0, "p", 1)
    for h in range(2):
        send(f"ix{h}", ipart(0, 0, h), ipart(1, 0, h), at(dh=1))
    ring_i(0, "m", 1)
    ring_i(0, "p", 0)

    dsum[0:R, :] = diag
    LO[0] = jnp.zeros((1, RP), jnp.float32)
    if RP > R:
        dsum[R:RP, :] = jnp.zeros((RP - R, 128), jnp.float32)
        for s in range(8):
            mr[s, R:RP, :] = jnp.zeros((RP - R, 128), jnp.float32)
            sr[s, R:RP, :] = jnp.ones((RP - R, 128), jnp.float32)
    for s in range(8):
        mr[s, 0:R, :] = jnp.full((R, 128), LOW, jnp.float32)
        sr[s, 0:R, :] = jnp.zeros((R, 128), jnp.float32)
    mc[...] = jnp.full(mc.shape, LOW, jnp.float32)
    sc[...] = jnp.zeros(sc.shape, jnp.float32)
    k = scale_ref[0]
    k2 = k * LOG2E

    def s_tile(a, lo, hi, first, last):
        rows, cols = slice(lo * R, hi * R), slice(first * Q, last * Q)
        tile = dot_nt(I[rows, :], T[a, cols, :]) * k2
        S[a, rows, cols] = tile
        parts = [tile[:, j : j + 128].reshape(hi - lo, R, 128) for j in range(0, (last - first) * Q, 128)]
        old = mr[lo:hi, 0:R, :]
        top = functools.reduce(jnp.maximum, parts, old)
        total = sr[lo:hi, 0:R, :] * jnp.exp2(old - top)
        for part in parts:
            total = total + jnp.exp2(part - top)
        mr[lo:hi, 0:R, :] = top
        sr[lo:hi, 0:R, :] = total
        by_col = tile.reshape((hi - lo) * R // 8, 8, (last - first) * Q)
        old = mc[a, :, cols]
        top = jnp.maximum(old, jnp.max(by_col, axis=0))
        sc[a, :, cols] = sc[a, :, cols] * jnp.exp2(old - top) + jnp.sum(jnp.exp2(by_col - top[None]), axis=0)
        mc[a, :, cols] = top

    on_t(0, "m")
    on_t(0, "p")
    on_i(0, "m")
    on_i(0, "p")
    got("tx0")
    ring_t(1, "m", 0)
    got("tx1")
    ring_t(1, "p", 1)
    ring_t(1, "m", 1)
    ring_t(1, "p", 0)
    to_core(0, 1)
    got("tzm01")
    to_core(3, 0)
    got("tzp00")
    to_core(1, 0)
    got("iym01", "iyp00", "tc00", "tc30", "tc10")
    s_tile(0, 0, 3, 0, 2)
    s_tile(0, 0, 3, 2, 3)
    got("thm0", "thp0")
    to_core(2, 0)
    got("ihm0", "ihp0", "ix0")
    ring_i(1, "m", 0)
    ring_i(1, "p", 0)
    s_tile(0, 3, 4, 0, 3)
    got("tc01")
    s_tile(1, 0, 4, 0, 1)
    got("ix1")
    ring_i(1, "m", 1)
    ring_i(1, "p", 1)
    on_t(1, "m")
    on_t(1, "p")
    got("tc20")
    s_tile(0, 0, 4, 3, 4)
    s_tile(0, 4, 5, 0, 4)
    got("tzm11")
    to_core(3, 1)
    got("tzp10")
    to_core(1, 1)
    on_i(1, "m")
    s_tile(1, 4, 5, 0, 1)
    got("tc31", "tc11")
    s_tile(1, 0, 5, 1, 3)
    on_i(1, "p")
    got("thm1", "thp1")
    to_core(2, 1)
    got("iym11", "iyp10")
    s_tile(0, 5, 7, 0, 2)
    s_tile(0, 5, 7, 2, 4)
    s_tile(1, 5, 7, 0, 3)
    got("tc21")
    s_tile(1, 0, 4, 3, 4)
    s_tile(1, 4, 7, 3, 4)
    def row_lse(s):
        m = mr[s].T
        top = jnp.max(m, axis=0, keepdims=True)
        total = jnp.sum(sr[s].T * jnp.exp2(m - top), axis=0, keepdims=True)
        LR[0, s : s + 1, :] = top + jnp.log(total) * LOG2E

    for s in range(7):
        row_lse(s)
    got("ihm1", "ihp1")
    s_tile(0, 7, 8, 0, 4)
    s_tile(1, 7, 8, 0, 4)
    for a in range(2):
        m = mc[a]
        top = jnp.max(m, axis=0, keepdims=True)
        total = jnp.sum(sc[a] * jnp.exp2(m - top), axis=0, keepdims=True)
        LC[0, a : a + 1, :] = top + jnp.log(total) * LOG2E
    for q, (r, a, b) in inner_peers:
        send(f"lc{q}", LC.at[0], LC.at[INNER.index((-r % 4, a, b))], at(dz=r, dl=a, dc=b))
    row_lse(7)
    for s, (a, r) in outer_peers:
        send(f"lr{s}", LR.at[0], LR.at[SLOT[a, -r % 4]], at(dh=a, dy=r))

    def merge(parts):
        top = functools.reduce(jnp.maximum, parts)
        total = functools.reduce(jnp.add, [jnp.exp2(part - top) for part in parts])
        return top + jnp.log(total) * LOG2E

    got(*[f"lc{q}" for q, _ in inner_peers])
    col_own = None
    for a in range(2):
        for g, r in enumerate(Z_OFF):
            parts = []
            for q, (dr, da, _) in enumerate(INNER):
                there = GROUP[(r - dr) % 4]
                parts.append(LC[q, (a ^ da) : (a ^ da) + 1, there * Q : (there + 1) * Q])
            lse = merge(parts)
            if a == 0 and g == 0:
                col_own = lse
            lcol[a, :, g * Q : (g + 1) * Q] = jnp.broadcast_to(lse + 1.0, (8, Q))
    got(*[f"lr{s}" for s, _ in outer_peers])
    row_own = None
    for s, (a, r) in enumerate(SLOTS):
        parts = []
        for p, (da, dr) in enumerate(SLOTS):
            there = SLOT[a ^ da, (r - dr) % 4]
            parts.append(LR[p, there : there + 1, :])
        lse = merge(parts)
        if s == 0:
            row_own = lse
        mr[s] = jnp.broadcast_to(lse + 1.0, (128, RP)).T

    def w_unit(a, g, slot):
        rows = slice(slot * R, (slot + 1) * R)
        by_row = mr[slot, 0:R, :]
        for j in range(g * Q, (g + 1) * Q, 128):
            cols = slice(j, j + 128)
            s = S[a, rows, cols]
            w = jnp.exp2(s - by_row) + jnp.exp2(s - lcol[a, 0:1, cols])
            W[a, rows, cols] = w.astype(jnp.bfloat16)

    done = set()

    def weights(needed):
        for unit in needed:
            if unit not in done:
                done.add(unit)
                w_unit(*unit)

    def for_t(a, g):
        return [(a, g, slot) for slot in range(8)]

    def for_i(slot):
        return [(a, g, slot) for a in range(2) for g in range(4)]

    def t_terms(a, g, then=()):
        weights(for_t(a, g))
        if a == 0:
            started[f"cs1{g}"].wait_send()
        weights(then)
        PT[g] = dot_tn(W[a, :, g * Q : (g + 1) * Q], I[...])
        send(f"cs{a}{g}", PT.at[g, pl.ds(core_row(1), R), :], CR.at[a, g], at(dc=1))

    def t_sum(a, g, h):
        rows = pl.ds(pl.multiple_of(core_row(0) + h * H, H), H)
        return PT[g, rows, :] + CR[a, g, h * H : (h + 1) * H, :]

    def i_terms(slot, then=()):
        weights(for_i(slot))
        weights(then)
        rows = slice(slot * R, (slot + 1) * R)
        return dot_nn(W[0, rows, :], T[0]) + dot_nn(W[1, rows, :], T[1])

    def far_t(a):
        got(f"cs{a}3")
        for i, d in enumerate("mp"):
            ZS[a, 0, i] = t_sum(a, 3, i).astype(jnp.bfloat16)
            send(f"zh{d}{a}", ZS.at[a, 0, i], ZH.at[a, i], at(dz=1 if d == "m" else 3))

    def far_i(a, then):
        term = i_terms(SLOT[a, 2], then)
        for i, d in enumerate("mp"):
            YS[a, 0, i] = term[i * H : (i + 1) * H].astype(jnp.bfloat16)
            send(f"yh{d}{a}", YS.at[a, 0, i], YH.at[a, i], at(dy=1 if d == "m" else 3))

    def z_send(a, i, h, part):
        ZS[a, 1 + i, h] = part.astype(jnp.bfloat16)
        send(f"zn{'mp'[i]}{a}{h}", ZS.at[a, 1 + i, h], ZN.at[a, i, h], at(dz=3 if i else 1))

    def y_send(a, i, h, part):
        YS[a, 1 + i, h] = part.astype(jnp.bfloat16)
        send(f"yn{'mp'[i]}{a}{h}", YS.at[a, 1 + i, h], YN.at[a, i, h], at(dy=3 if i else 1))

    def near_t(a, i):
        g = GROUP[3 if i else 1]
        if (a, i) != (1, 1):
            got(f"cs{a}{g}")
        z_send(a, i, 1 - i, t_sum(a, g, 1 - i))

    def near_t_met(a, i):
        g = GROUP[3 if i else 1]
        if (a, i) == (1, 1):
            got(f"cs{a}{g}")
        got(f"zh{'mp'[i]}{a}")
        z_send(a, i, i, t_sum(a, g, i) + ZH[a, i].astype(jnp.float32))

    def near_i(a, i, then):
        term = i_terms(SLOT[a, 3 if i else 1], then)
        y_send(a, i, 1 - i, term[(1 - i) * H : (2 - i) * H])
        KI[i] = term[i * H : (i + 1) * H]

    def near_i_met(a, i):
        got(f"yh{'mp'[i]}{a}")
        y_send(a, i, i, KI[i] + YH[a, i].astype(jnp.float32))

    def ring_sum(name, held, a, h, term):
        got(f"{name}m{a}{h}", f"{name}p{a}{h}")
        return term + (held[a, 0, h].astype(jnp.float32) + held[a, 1, h].astype(jnp.float32))

    halves = [(h, slice(h * H, (h + 1) * H)) for h in range(2)]
    t_terms(1, 3)
    t_terms(1, 1)
    far_t(1)
    t_terms(1, 2, for_i(SLOT[1, 2]))
    near_t(1, 0)
    far_i(1, for_t(1, 0))

    col_mine = jnp.where(c == 0, col_own[:, 0:R], col_own[:, R:Q])
    diag_own = jnp.sum(dsum[...].T, axis=0, keepdims=True) * k2
    LO[0, :, 0:R] = row_own[:, 0:R] + col_mine - 2.0 * diag_own[:, 0:R]
    for s, (a, r) in outer_peers:
        send(f"lo{s}", LO.at[0], LO.at[SLOT[a, -r % 4]], at(dh=a, dy=r))


    def across_t(h):
        rows = halves[h][1]
        XS[0, rows, :] = ring_sum("zn", ZN, 1, h, t_sum(1, 0, h)).astype(jnp.bfloat16)
        send(f"xs{h}", XS.at[0, rows, :], XR.at[0, rows, :], at(dl=1))

    def across_i(h):
        rows = halves[h][1]
        XS[1, rows, :] = ring_sum("yn", YN, 1, h, ig_ref[rows, :]).astype(jnp.bfloat16)
        send(f"xi{h}", XS.at[1, rows, :], XR.at[1, rows, :], at(dh=1))

    t_terms(1, 0, for_i(SLOT[1, 1]))
    near_t_met(1, 1)
    near_t(1, 1)
    near_t_met(1, 0)
    near_i(1, 0, for_i(SLOT[1, 3]))
    near_i(1, 1, for_t(0, 3))
    near_i_met(1, 0)
    near_i_met(1, 1)
    t_terms(0, 3, for_i(SLOT[1, 0]))
    got("cs10")
    across_t(1)

    def ring(values):
        return (values[0] + values[2]) + (values[1] + values[3])

    got(*[f"lo{s}" for s, _ in outer_peers])
    LI[0] = ring([LO[SLOT[0, r]] for r in range(4)]) + ring([LO[SLOT[1, r]] for r in range(4)])
    for q, (r, a, b) in inner_peers:
        send(f"li{q}", LI.at[0], LI.at[INNER.index((-r % 4, a, b))], at(dz=r, dl=a, dc=b))

    ig_ref[...] = i_terms(SLOT[1, 0], for_i(SLOT[0, 2]))
    far_t(0)
    far_i(0, for_t(0, 1))
    across_t(0)
    t_terms(0, 1, for_t(0, 2))
    t_terms(0, 2, for_i(SLOT[0, 1]))
    near_t(0, 0)
    near_t(0, 1)
    across_i(0)
    across_i(1)
    near_i(0, 0, for_i(SLOT[0, 3]))
    near_i(0, 1, for_t(0, 0))
    near_t_met(0, 0)
    near_t_met(0, 1)
    near_i_met(0, 0)
    near_i_met(0, 1)
    t_terms(0, 0, for_i(SLOT[0, 0]))
    ig_ref[...] = i_terms(SLOT[0, 0])
    got("cs00")
    for h, rows in halves:
        tg_ref[rows, :] = ring_sum("zn", ZN, 0, h, t_sum(0, 0, h)) - I[rows, :].astype(jnp.float32)
    for h, rows in halves:
        text = T[0, trows(0, 0, h), :].astype(jnp.float32)
        ig_ref[rows, :] = ring_sum("yn", YN, 0, h, ig_ref[rows, :]) - text

    got(*[f"li{q}" for q, _ in inner_peers])
    by_z = []
    for r in range(4):
        v = [[LI[INNER.index((r, a, b))] for b in range(2)] for a in range(2)]
        by_z.append((v[0][0] + v[0][1]) + (v[1][0] + v[1][1]))
    loss_ref[...] = jnp.sum(ring(by_z)[:, 0:R], axis=1, keepdims=True) * (LN2 / (2 * 128 * R))

    for h in range(2):
        rows = slice(h * H, (h + 1) * H)
        got(f"xs{h}")
        tg_ref[rows, :] = k * (tg_ref[rows, :] + XR[0, rows, :].astype(jnp.float32))
    text_out = pltpu.make_async_copy(tg_ref, tg_hbm, own_sems.at[2])
    text_out.start()
    image_out = []
    for h in range(2):
        rows = slice(h * H, (h + 1) * H)
        got(f"xi{h}")
        ig_ref[rows, :] = k * (ig_ref[rows, :] + XR[1, rows, :].astype(jnp.float32))
        image_out.append(pltpu.make_async_copy(ig_ref.at[rows, :], ig_hbm.at[rows, :], own_sems.at[3 + h]))
        image_out[h].start()
    text_out.wait()
    for copy in image_out:
        copy.wait()
    for name in started:
        if not name.startswith("cs1"):
            started[name].wait_send()


def hand_over(ig_ref, tg_ref, ig_out, tg_out):
    ig_out[...] = ig_ref[...]
    tg_out[...] = tg_ref[...]


def per_device(image_codes, image_exps, text_codes, text_exps, logit_scale):
    R, D = image_codes.shape
    H = R // 2
    C = 8 * R
    RP = -(-R // 128) * 128
    bf16, f32 = jnp.bfloat16, jnp.float32
    vmem = pl.BlockSpec(memory_space=pltpu.VMEM)
    hbm = pl.BlockSpec(memory_space=pl.ANY)
    scratch = [
        pltpu.VMEM((2, C, D), bf16),
        pltpu.VMEM((C, D), bf16),
        pltpu.VMEM((2, C, C), f32),
        pltpu.VMEM((2, C, C), bf16),
        pltpu.VMEM((8, RP, 128), f32),
        pltpu.VMEM((8, RP, 128), f32),
        pltpu.VMEM((2, 8, C), f32),
        pltpu.VMEM((2, 8, C), f32),
        pltpu.VMEM((2, 8, C), f32),
        pltpu.VMEM((8, 8, RP), f32),
        pltpu.VMEM((16, 2, C), f32),
        pltpu.VMEM((8, 1, RP), f32),
        pltpu.VMEM((16, 1, RP), f32),
        pltpu.VMEM((4, 2 * R, D), f32),
        pltpu.VMEM((2, 4, R, D), f32),
        pltpu.VMEM((2, 3, 2, H, D), bf16),
        pltpu.VMEM((2, 2, H, D), bf16),
        pltpu.VMEM((2, 2, 2, H, D), bf16),
        pltpu.VMEM((2, 3, 2, H, D), bf16),
        pltpu.VMEM((2, 2, H, D), bf16),
        pltpu.VMEM((2, 2, 2, H, D), bf16),
        pltpu.VMEM((2, H, D), f32),
        pltpu.VMEM((2, R, D), bf16),
        pltpu.VMEM((2, R, D), bf16),
        pltpu.VMEM((RP, 128), f32),
        pltpu.VMEM((128, RP), jnp.int32),
        pltpu.VMEM((2, R, D), jnp.int32),
        pltpu.VMEM((2, R, D), f32),
        pltpu.SemaphoreType.DMA((5,)),
        pltpu.SemaphoreType.DMA((len(MESSAGES),)),
        pltpu.SemaphoreType.DMA((len(MESSAGES),)),
    ]
    loss, image_grad, text_grad = pl.pallas_call(
        kernel,
        out_shape=[
            jax.ShapeDtypeStruct((1, 1), f32),
            jax.ShapeDtypeStruct((R, D), f32),
            jax.ShapeDtypeStruct((R, D), f32),
        ],
        in_specs=[hbm, vmem, hbm, vmem, pl.BlockSpec(memory_space=pltpu.SMEM)],
        out_specs=[vmem, hbm, hbm],
        scratch_shapes=scratch,
        compiler_params=pltpu.CompilerParams(
            collective_id=0, has_side_effects=True, vmem_limit_bytes=63 * 1024 * 1024
        ),
    )(image_codes, image_exps.T, text_codes, text_exps.T, logit_scale)
    image_grad, text_grad = pl.pallas_call(
        hand_over,
        out_shape=[jax.ShapeDtypeStruct((R, D), f32)] * 2,
        in_specs=[vmem] * 2,
        out_specs=[vmem] * 2,
    )(image_grad, text_grad)
    return loss.reshape(()), image_grad, text_grad


def solution(mesh):
    rows = P(("outer", "inner"), None)
    return jax.shard_map(
        per_device, mesh=mesh, in_specs=(rows, rows, rows, rows, P()), out_specs=(P(), rows, rows), check_vma=False
    )
```

```python
import functools

import jax
import jax.numpy as jnp
from jax import lax
from jax.experimental import pallas as pl
from jax.experimental.pallas import tpu as pltpu
from jax.sharding import PartitionSpec as P

LOG2E = 1.4426950408889634
LN2 = 0.6931471805599453
UNIT = 2.0 ** -17
LOW = -1e30
Z_OFF = (0, 1, 3, 2)
GROUP = {off: g for g, off in enumerate(Z_OFF)}
SLOTS = ((0, 0), (0, 1), (0, 3), (0, 2), (1, 0), (1, 1), (1, 3), (1, 2))
SLOT = {pos: s for s, pos in enumerate(SLOTS)}
INNER = [(r, a, b) for r in range(4) for a in range(2) for b in range(2)]
MESH = pl.DeviceIdType.MESH
MESSAGES = (
    [f"{n}{h}" for n in ("tx", "ix", "xs", "xi") for h in range(2)]
    + [f"tc{r}{a}" for r in range(4) for a in range(2)]
    + [f"{n}{d}{a}{h}" for n in ("tz", "iy", "zn", "yn") for d in "pm" for a in range(2) for h in range(2)]
    + [f"{n}{d}{a}" for n in ("th", "ih", "zh", "yh") for d in "pm" for a in range(2)]
    + [f"cs{a}{g}" for a in range(2) for g in range(4)]
    + [f"{n}{s}" for n in ("lr", "lo") for s in range(1, 8)]
    + [f"{n}{q}" for n in ("lc", "li") for q in range(1, 16)]
)
SEM = {name: i for i, name in enumerate(MESSAGES)}


def dot_nt(a, b):
    return lax.dot_general(a, b, (((1,), (1,)), ((), ())), preferred_element_type=jnp.float32)


def dot_nn(a, b):
    return jnp.dot(a, b, preferred_element_type=jnp.float32)


def dot_tn(a, b):
    return lax.dot_general(a, b, (((0,), (0,)), ((), ())), preferred_element_type=jnp.float32)


def kernel(
    ic_hbm, ie_ref, tc_hbm, te_ref, scale_ref, loss_ref, ig_hbm, tg_hbm,
    T, I, S, W, mr, sr, mc, sc, lcol, LR, LC, LO, LI,
    PT, CR, ZS, ZH, ZN, YS, YH, YN, KI, XS, XR, dsum, exps, codes, grads, own_sems, send_sems, recv_sems,
):
    R, D = ic_hbm.shape
    ic_ref, tc_ref = codes.at[0], codes.at[1]
    ig_ref, tg_ref = grads.at[0], grads.at[1]
    H = R // 2
    Q = 2 * R
    C = 8 * R
    RP = LR.shape[2]
    ND = D // 128
    NB = ie_ref.shape[0]

    outer = lax.axis_index("outer")
    inner = lax.axis_index("inner")
    xh, y = outer // 4, outer % 4
    z, xl, c = inner // 4, (inner // 2) % 2, inner % 2

    def at(dh=0, dy=0, dz=0, dl=0, dc=0):
        h = xh if dh == 0 else 1 - xh
        l = xl if dl == 0 else 1 - xl
        k = c if dc == 0 else 1 - c
        return (h * 4 + (y + dy) % 4, ((z + dz) % 4) * 4 + l * 2 + k)

    outer_peers = [(s, SLOTS[s]) for s in range(1, 8)]
    inner_peers = [(q, INNER[q]) for q in range(1, 16)]
    barrier = pltpu.get_barrier_semaphore()
    for _, (a, r) in outer_peers:
        pl.semaphore_signal(barrier, inc=1, device_id=at(dh=a, dy=r), device_id_type=MESH)
    for _, (r, a, b) in inner_peers:
        pl.semaphore_signal(barrier, inc=1, device_id=at(dz=r, dl=a, dc=b), device_id_type=MESH)
    text_in = pltpu.make_async_copy(tc_hbm, tc_ref, own_sems.at[0])
    image_in = pltpu.make_async_copy(ic_hbm, ic_ref, own_sems.at[1])
    text_in.start()
    image_in.start()

    started = {}

    def send(name, src, dst, device):
        started[name] = pltpu.make_async_remote_copy(
            src_ref=src, dst_ref=dst, send_sem=send_sems.at[SEM[name]], recv_sem=recv_sems.at[SEM[name]],
            device_id=device, device_id_type=MESH,
        )
        started[name].start()

    def got(*names):
        for name in names:
            started[name].wait_recv()

    def core_row(b):
        return pl.multiple_of((c if b == 0 else 1 - c) * R, R)

    def trows(r, b, h=None):
        first = GROUP[r] * Q + core_row(b)
        if h is None:
            return pl.ds(pl.multiple_of(first, R), R)
        return pl.ds(pl.multiple_of(first + h * H, H), H)

    def tpart(a, r, h=None):
        return T.at[a, trows(r, 0, h), :]

    def ipart(a, r, h):
        return I.at[pl.ds(SLOT[a, r] * R + h * H, H), :]

    def columns(exps_ref):
        exps[0:NB, 0:R] = exps_ref[...]
        return exps[...].T

    def decode(codes_ref, exps_by_row, f):
        codes = codes_ref[:, f * 128 : (f + 1) * 128]
        field = (codes >> 3) & 15
        mantissa = codes & 7
        significand = jnp.where(field > 0, mantissa + 8, mantissa)
        shift = jnp.maximum(field, 1) - 1 + (exps_by_row[0:R, f : f + 1] + 8)
        magnitude = (significand << shift).astype(jnp.float32) * UNIT
        return jnp.where(codes > 127, -magnitude, magnitude)

    exps[...] = jnp.zeros(exps.shape, jnp.int32)
    image_exps = columns(ie_ref)
    text_exps = columns(te_ref)
    text_in.wait()
    for f in range(ND):
        text = decode(tc_ref, text_exps, f)
        T[0, trows(0, 0), f * 128 : (f + 1) * 128] = text.astype(jnp.bfloat16)

    pl.semaphore_wait(barrier, 22)

    def ring_t(a, d, h):
        far = 1 if d == "m" else 3
        send(f"tz{d}{a}{h}", tpart(a, 0, h), tpart(a, -far % 4, h), at(dz=far))

    def ring_i(a, d, h):
        far = 1 if d == "m" else 3
        send(f"iy{d}{a}{h}", ipart(a, 0, h), ipart(a, -far % 4, h), at(dy=far))

    def on_t(a, d):
        far, h = (1, 0) if d == "m" else (3, 1)
        got(f"tz{d}{a}{h}")
        send(f"th{d}{a}", tpart(a, -far % 4, h), tpart(a, 2, h), at(dz=far))

    def on_i(a, d):
        far, h = (1, 0) if d == "m" else (3, 1)
        got(f"iy{d}{a}{h}")
        send(f"ih{d}{a}", ipart(a, -far % 4, h), ipart(a, 2, h), at(dy=far))

    def to_core(r, a):
        send(f"tc{r}{a}", tpart(a, r), tpart(a, r), at(dc=1))

    ring_t(0, "m", 0)
    ring_t(0, "p", 1)
    for h in range(2):
        send(f"tx{h}", tpart(0, 0, h), tpart(1, 0, h), at(dl=1))
    ring_t(0, "m", 1)
    ring_t(0, "p", 0)
    to_core(0, 0)
    image_in.wait()
    diag = jnp.zeros((R, 128), jnp.float32)
    for f in range(ND):
        image = decode(ic_ref, image_exps, f)
        diag = diag + image * T[0, trows(0, 0), f * 128 : (f + 1) * 128].astype(jnp.float32)
        I[0:R, f * 128 : (f + 1) * 128] = image.astype(jnp.bfloat16)
    ring_i(0, "m", 0)
    ring_i(0, "p", 1)
    for h in range(2):
        send(f"ix{h}", ipart(0, 0, h), ipart(1, 0, h), at(dh=1))
    ring_i(0, "m", 1)
    ring_i(0, "p", 0)

    dsum[0:R, :] = diag
    LO[0] = jnp.zeros((1, RP), jnp.float32)
    if RP > R:
        dsum[R:RP, :] = jnp.zeros((RP - R, 128), jnp.float32)
        for s in range(8):
            mr[s, R:RP, :] = jnp.zeros((RP - R, 128), jnp.float32)
            sr[s, R:RP, :] = jnp.ones((RP - R, 128), jnp.float32)
    for s in range(8):
        mr[s, 0:R, :] = jnp.full((R, 128), LOW, jnp.float32)
        sr[s, 0:R, :] = jnp.zeros((R, 128), jnp.float32)
    mc[...] = jnp.full(mc.shape, LOW, jnp.float32)
    sc[...] = jnp.zeros(sc.shape, jnp.float32)
    k = scale_ref[0]
    k2 = k * LOG2E

    def s_tile(a, lo, hi, first, last):
        rows, cols = slice(lo * R, hi * R), slice(first * Q, last * Q)
        tile = dot_nt(I[rows, :], T[a, cols, :]) * k2
        S[a, rows, cols] = tile
        parts = [tile[:, j : j + 128].reshape(hi - lo, R, 128) for j in range(0, (last - first) * Q, 128)]
        old = mr[lo:hi, 0:R, :]
        top = functools.reduce(jnp.maximum, parts, old)
        total = sr[lo:hi, 0:R, :] * jnp.exp2(old - top)
        for part in parts:
            total = total + jnp.exp2(part - top)
        mr[lo:hi, 0:R, :] = top
        sr[lo:hi, 0:R, :] = total
        by_col = tile.reshape((hi - lo) * R // 8, 8, (last - first) * Q)
        old = mc[a, :, cols]
        top = jnp.maximum(old, jnp.max(by_col, axis=0))
        sc[a, :, cols] = sc[a, :, cols] * jnp.exp2(old - top) + jnp.sum(jnp.exp2(by_col - top[None]), axis=0)
        mc[a, :, cols] = top

    on_t(0, "m")
    on_t(0, "p")
    on_i(0, "m")
    on_i(0, "p")
    got("tx0")
    ring_t(1, "m", 0)
    got("tx1")
    ring_t(1, "p", 1)
    ring_t(1, "m", 1)
    ring_t(1, "p", 0)
    to_core(0, 1)
    got("tzm01")
    to_core(3, 0)
    got("tzp00")
    to_core(1, 0)
    got("iym01", "iyp00", "tc00", "tc30", "tc10")
    s_tile(0, 0, 3, 0, 2)
    s_tile(0, 0, 3, 2, 3)
    got("thm0", "thp0")
    to_core(2, 0)
    got("ihm0", "ihp0", "ix0")
    ring_i(1, "m", 0)
    ring_i(1, "p", 0)
    s_tile(0, 3, 4, 0, 3)
    got("tc01")
    s_tile(1, 0, 4, 0, 1)
    got("ix1")
    ring_i(1, "m", 1)
    ring_i(1, "p", 1)
    on_t(1, "m")
    on_t(1, "p")
    got("tc20")
    s_tile(0, 0, 4, 3, 4)
    s_tile(0, 4, 5, 0, 4)
    got("tzm11")
    to_core(3, 1)
    got("tzp10")
    to_core(1, 1)
    on_i(1, "m")
    s_tile(1, 4, 5, 0, 1)
    got("tc31", "tc11")
    s_tile(1, 0, 5, 1, 2)
    on_i(1, "p")
    s_tile(1, 0, 5, 2, 3)
    got("thm1", "thp1")
    to_core(2, 1)
    got("iym11", "iyp10")
    s_tile(0, 5, 7, 0, 2)
    s_tile(0, 5, 7, 2, 4)
    s_tile(1, 5, 7, 0, 3)
    got("tc21")
    s_tile(1, 0, 4, 3, 4)
    s_tile(1, 4, 7, 3, 4)
    def row_lse(s):
        m = mr[s].T
        top = jnp.max(m, axis=0, keepdims=True)
        total = jnp.sum(sr[s].T * jnp.exp2(m - top), axis=0, keepdims=True)
        LR[0, s : s + 1, :] = top + jnp.log(total) * LOG2E

    for s in range(7):
        row_lse(s)
    got("ihm1", "ihp1")
    s_tile(0, 7, 8, 0, 4)
    s_tile(1, 7, 8, 0, 4)
    for a in range(2):
        m = mc[a]
        top = jnp.max(m, axis=0, keepdims=True)
        total = jnp.sum(sc[a] * jnp.exp2(m - top), axis=0, keepdims=True)
        LC[0, a : a + 1, :] = top + jnp.log(total) * LOG2E
    for q, (r, a, b) in inner_peers:
        send(f"lc{q}", LC.at[0], LC.at[INNER.index((-r % 4, a, b))], at(dz=r, dl=a, dc=b))
    row_lse(7)
    for s, (a, r) in outer_peers:
        send(f"lr{s}", LR.at[0], LR.at[SLOT[a, -r % 4]], at(dh=a, dy=r))

    def merge(parts):
        top = functools.reduce(jnp.maximum, parts)
        total = functools.reduce(jnp.add, [jnp.exp2(part - top) for part in parts])
        return top + jnp.log(total) * LOG2E

    got(*[f"lc{q}" for q, _ in inner_peers])
    col_own = None
    for a in range(2):
        for g, r in enumerate(Z_OFF):
            parts = []
            for q, (dr, da, _) in enumerate(INNER):
                there = GROUP[(r - dr) % 4]
                parts.append(LC[q, (a ^ da) : (a ^ da) + 1, there * Q : (there + 1) * Q])
            lse = merge(parts)
            if a == 0 and g == 0:
                col_own = lse
            lcol[a, :, g * Q : (g + 1) * Q] = jnp.broadcast_to(lse + 1.0, (8, Q))
    got(*[f"lr{s}" for s, _ in outer_peers])
    row_own = None
    for s, (a, r) in enumerate(SLOTS):
        parts = []
        for p, (da, dr) in enumerate(SLOTS):
            there = SLOT[a ^ da, (r - dr) % 4]
            parts.append(LR[p, there : there + 1, :])
        lse = merge(parts)
        if s == 0:
            row_own = lse
        mr[s] = jnp.broadcast_to(lse + 1.0, (128, RP)).T

    def w_unit(a, g, slot):
        rows = slice(slot * R, (slot + 1) * R)
        by_row = mr[slot, 0:R, :]
        for j in range(g * Q, (g + 1) * Q, 128):
            cols = slice(j, j + 128)
            s = S[a, rows, cols]
            w = jnp.exp2(s - by_row) + jnp.exp2(s - lcol[a, 0:1, cols])
            W[a, rows, cols] = w.astype(jnp.bfloat16)

    done = set()

    def weights(needed):
        for unit in needed:
            if unit not in done:
                done.add(unit)
                w_unit(*unit)

    def for_t(a, g):
        return [(a, g, slot) for slot in range(8)]

    def for_i(slot):
        return [(a, g, slot) for a in range(2) for g in range(4)]

    def t_terms(a, g, then=()):
        weights(for_t(a, g))
        if a == 0:
            started[f"cs1{g}"].wait_send()
        weights(then)
        PT[g] = dot_tn(W[a, :, g * Q : (g + 1) * Q], I[...])
        send(f"cs{a}{g}", PT.at[g, pl.ds(core_row(1), R), :], CR.at[a, g], at(dc=1))

    def t_sum(a, g, h):
        rows = pl.ds(pl.multiple_of(core_row(0) + h * H, H), H)
        return PT[g, rows, :] + CR[a, g, h * H : (h + 1) * H, :]

    def i_terms(slot, then=()):
        weights(for_i(slot))
        weights(then)
        rows = slice(slot * R, (slot + 1) * R)
        return dot_nn(W[0, rows, :], T[0]) + dot_nn(W[1, rows, :], T[1])

    def far_t(a):
        got(f"cs{a}3")
        for i, d in enumerate("mp"):
            ZS[a, 0, i] = t_sum(a, 3, i).astype(jnp.bfloat16)
            send(f"zh{d}{a}", ZS.at[a, 0, i], ZH.at[a, i], at(dz=1 if d == "m" else 3))

    def far_i(a, then):
        term = i_terms(SLOT[a, 2], then)
        for i, d in enumerate("mp"):
            YS[a, 0, i] = term[i * H : (i + 1) * H].astype(jnp.bfloat16)
            send(f"yh{d}{a}", YS.at[a, 0, i], YH.at[a, i], at(dy=1 if d == "m" else 3))

    def z_send(a, i, h, part):
        ZS[a, 1 + i, h] = part.astype(jnp.bfloat16)
        send(f"zn{'mp'[i]}{a}{h}", ZS.at[a, 1 + i, h], ZN.at[a, i, h], at(dz=3 if i else 1))

    def y_send(a, i, h, part):
        YS[a, 1 + i, h] = part.astype(jnp.bfloat16)
        send(f"yn{'mp'[i]}{a}{h}", YS.at[a, 1 + i, h], YN.at[a, i, h], at(dy=3 if i else 1))

    def near_t(a, i):
        g = GROUP[3 if i else 1]
        if (a, i) != (1, 1):
            got(f"cs{a}{g}")
        z_send(a, i, 1 - i, t_sum(a, g, 1 - i))

    def near_t_met(a, i):
        g = GROUP[3 if i else 1]
        if (a, i) == (1, 1):
            got(f"cs{a}{g}")
        got(f"zh{'mp'[i]}{a}")
        z_send(a, i, i, t_sum(a, g, i) + ZH[a, i].astype(jnp.float32))

    def near_i(a, i, then):
        term = i_terms(SLOT[a, 3 if i else 1], then)
        y_send(a, i, 1 - i, term[(1 - i) * H : (2 - i) * H])
        KI[i] = term[i * H : (i + 1) * H]

    def near_i_met(a, i):
        got(f"yh{'mp'[i]}{a}")
        y_send(a, i, i, KI[i] + YH[a, i].astype(jnp.float32))

    def ring_sum(name, held, a, h, term):
        got(f"{name}m{a}{h}", f"{name}p{a}{h}")
        return term + (held[a, 0, h].astype(jnp.float32) + held[a, 1, h].astype(jnp.float32))

    halves = [(h, slice(h * H, (h + 1) * H)) for h in range(2)]
    t_terms(1, 3)
    t_terms(1, 1)
    far_t(1)
    t_terms(1, 2, for_i(SLOT[1, 2]))
    near_t(1, 0)
    far_i(1, for_t(1, 0))

    col_mine = jnp.where(c == 0, col_own[:, 0:R], col_own[:, R:Q])
    diag_own = jnp.sum(dsum[...].T, axis=0, keepdims=True) * k2
    LO[0, :, 0:R] = row_own[:, 0:R] + col_mine - 2.0 * diag_own[:, 0:R]
    for s, (a, r) in outer_peers:
        send(f"lo{s}", LO.at[0], LO.at[SLOT[a, -r % 4]], at(dh=a, dy=r))


    def across_t(h):
        rows = halves[h][1]
        XS[0, rows, :] = ring_sum("zn", ZN, 1, h, t_sum(1, 0, h)).astype(jnp.bfloat16)
        send(f"xs{h}", XS.at[0, rows, :], XR.at[0, rows, :], at(dl=1))

    def across_i(h):
        rows = halves[h][1]
        XS[1, rows, :] = ring_sum("yn", YN, 1, h, ig_ref[rows, :]).astype(jnp.bfloat16)
        send(f"xi{h}", XS.at[1, rows, :], XR.at[1, rows, :], at(dh=1))

    t_terms(1, 0, for_i(SLOT[1, 1]))
    near_t_met(1, 1)
    near_t(1, 1)
    near_t_met(1, 0)
    near_i(1, 0, for_i(SLOT[1, 3]))
    near_i(1, 1, for_t(0, 3))
    near_i_met(1, 0)
    near_i_met(1, 1)
    t_terms(0, 3, for_i(SLOT[1, 0]))
    got("cs10")
    across_t(1)

    def ring(values):
        return (values[0] + values[2]) + (values[1] + values[3])

    got(*[f"lo{s}" for s, _ in outer_peers])
    LI[0] = ring([LO[SLOT[0, r]] for r in range(4)]) + ring([LO[SLOT[1, r]] for r in range(4)])
    for q, (r, a, b) in inner_peers:
        send(f"li{q}", LI.at[0], LI.at[INNER.index((-r % 4, a, b))], at(dz=r, dl=a, dc=b))

    ig_ref[...] = i_terms(SLOT[1, 0], for_i(SLOT[0, 2]))
    far_t(0)
    far_i(0, for_t(0, 1))
    across_t(0)
    t_terms(0, 1, for_t(0, 2))
    t_terms(0, 2, for_i(SLOT[0, 1]))
    near_t(0, 0)
    near_t(0, 1)
    across_i(0)
    across_i(1)
    near_i(0, 0, for_i(SLOT[0, 3]))
    near_i(0, 1, for_t(0, 0))
    near_t_met(0, 0)
    near_t_met(0, 1)
    near_i_met(0, 0)
    near_i_met(0, 1)
    t_terms(0, 0, for_i(SLOT[0, 0]))
    ig_ref[...] = i_terms(SLOT[0, 0])
    got("cs00")
    for h, rows in halves:
        tg_ref[rows, :] = ring_sum("zn", ZN, 0, h, t_sum(0, 0, h)) - I[rows, :].astype(jnp.float32)
    for h, rows in halves:
        text = T[0, trows(0, 0, h), :].astype(jnp.float32)
        ig_ref[rows, :] = ring_sum("yn", YN, 0, h, ig_ref[rows, :]) - text

    got(*[f"li{q}" for q, _ in inner_peers])
    by_z = []
    for r in range(4):
        v = [[LI[INNER.index((r, a, b))] for b in range(2)] for a in range(2)]
        by_z.append((v[0][0] + v[0][1]) + (v[1][0] + v[1][1]))
    loss_ref[...] = jnp.sum(ring(by_z)[:, 0:R], axis=1, keepdims=True) * (LN2 / (2 * 128 * R))

    for h in range(2):
        rows = slice(h * H, (h + 1) * H)
        got(f"xs{h}")
        tg_ref[rows, :] = k * (tg_ref[rows, :] + XR[0, rows, :].astype(jnp.float32))
    text_out = pltpu.make_async_copy(tg_ref, tg_hbm, own_sems.at[2])
    text_out.start()
    image_out = []
    for h in range(2):
        rows = slice(h * H, (h + 1) * H)
        got(f"xi{h}")
        ig_ref[rows, :] = k * (ig_ref[rows, :] + XR[1, rows, :].astype(jnp.float32))
        image_out.append(pltpu.make_async_copy(ig_ref.at[rows, :], ig_hbm.at[rows, :], own_sems.at[3 + h]))
        image_out[h].start()
    text_out.wait()
    for copy in image_out:
        copy.wait()
    for name in started:
        if not name.startswith("cs1"):
            started[name].wait_send()


def hand_over(ig_ref, tg_ref, ig_out, tg_out):
    ig_out[...] = ig_ref[...]
    tg_out[...] = tg_ref[...]


def per_device(image_codes, image_exps, text_codes, text_exps, logit_scale):
    R, D = image_codes.shape
    H = R // 2
    C = 8 * R
    RP = -(-R // 128) * 128
    bf16, f32 = jnp.bfloat16, jnp.float32
    vmem = pl.BlockSpec(memory_space=pltpu.VMEM)
    hbm = pl.BlockSpec(memory_space=pl.ANY)
    scratch = [
        pltpu.VMEM((2, C, D), bf16),
        pltpu.VMEM((C, D), bf16),
        pltpu.VMEM((2, C, C), f32),
        pltpu.VMEM((2, C, C), bf16),
        pltpu.VMEM((8, RP, 128), f32),
        pltpu.VMEM((8, RP, 128), f32),
        pltpu.VMEM((2, 8, C), f32),
        pltpu.VMEM((2, 8, C), f32),
        pltpu.VMEM((2, 8, C), f32),
        pltpu.VMEM((8, 8, RP), f32),
        pltpu.VMEM((16, 2, C), f32),
        pltpu.VMEM((8, 1, RP), f32),
        pltpu.VMEM((16, 1, RP), f32),
        pltpu.VMEM((4, 2 * R, D), f32),
        pltpu.VMEM((2, 4, R, D), f32),
        pltpu.VMEM((2, 3, 2, H, D), bf16),
        pltpu.VMEM((2, 2, H, D), bf16),
        pltpu.VMEM((2, 2, 2, H, D), bf16),
        pltpu.VMEM((2, 3, 2, H, D), bf16),
        pltpu.VMEM((2, 2, H, D), bf16),
        pltpu.VMEM((2, 2, 2, H, D), bf16),
        pltpu.VMEM((2, H, D), f32),
        pltpu.VMEM((2, R, D), bf16),
        pltpu.VMEM((2, R, D), bf16),
        pltpu.VMEM((RP, 128), f32),
        pltpu.VMEM((128, RP), jnp.int32),
        pltpu.VMEM((2, R, D), jnp.int32),
        pltpu.VMEM((2, R, D), f32),
        pltpu.SemaphoreType.DMA((5,)),
        pltpu.SemaphoreType.DMA((len(MESSAGES),)),
        pltpu.SemaphoreType.DMA((len(MESSAGES),)),
    ]
    loss, image_grad, text_grad = pl.pallas_call(
        kernel,
        out_shape=[
            jax.ShapeDtypeStruct((1, 1), f32),
            jax.ShapeDtypeStruct((R, D), f32),
            jax.ShapeDtypeStruct((R, D), f32),
        ],
        in_specs=[hbm, vmem, hbm, vmem, pl.BlockSpec(memory_space=pltpu.SMEM)],
        out_specs=[vmem, hbm, hbm],
        scratch_shapes=scratch,
        compiler_params=pltpu.CompilerParams(
            collective_id=0, has_side_effects=True, vmem_limit_bytes=63 * 1024 * 1024
        ),
    )(image_codes, image_exps.T, text_codes, text_exps.T, logit_scale)
    image_grad, text_grad = pl.pallas_call(
        hand_over,
        out_shape=[jax.ShapeDtypeStruct((R, D), f32)] * 2,
        in_specs=[vmem] * 2,
        out_specs=[vmem] * 2,
    )(image_grad, text_grad)
    return loss.reshape(()), image_grad, text_grad


def solution(mesh):
    rows = P(("outer", "inner"), None)
    return jax.shard_map(
        per_device, mesh=mesh, in_specs=(rows, rows, rows, rows, P()), out_specs=(P(), rows, rows), check_vma=False
    )
```
